256 devices in a mesh: dp: 8 (over x, core), seq: 32 (over z, y).
Axes of the slice: x: 4, y: 4, z: 8, core: 2. Of those that a mesh axis runs over, the one named last changes fastest.
Arguments:
- queries: bfloat16 [8, 32, 512, 512], P('dp', 'seq'), may hold values from -8 to 8
- keys: bfloat16 [8, 32, 512, 128], P('dp', 'seq'), may hold values from -8 to 8
- values: bfloat16 [8, 32, 512, 128], P('dp', 'seq'), may hold values from -6 to 6
- grad_out: bfloat16 [8, 32, 512, 4096], P('dp', 'seq'), may hold values from -6 to 6
- out_weight: bfloat16 [4096, 512], P('dp'), may hold values from -0.25 to 0.25
- ancestors: int32 [8, 32, 3], P('dp'), may hold values from -1 to 30, as said below
- owner: int32 [8, 32], P('dp'), may hold values from 0 to 31, each once within a row
- lengths: int32 [8, 32], P('dp'), may hold values from 128 to 512, as said below
Outputs:
- grad_queries: bfloat16 [8, 32, 512, 512], P('dp', 'seq')
- grad_keys: bfloat16 [8, 32, 512, 128], P('dp', 'seq')
- grad_values: bfloat16 [8, 32, 512, 128], P('dp', 'seq')
- grad_weight: float32 [4096, 512], P(('dp', 'seq'))
The draws below stay inside these ranges and needn't reach their ends.
Inputs may be any that keep to these rules, and one draw needn't show every extreme that they name: Row n lists node n's ancestors root first, each the parent of the next and the last the parent of n, then -1 in the places left; every ancestor has a smaller id than n; node 0 is the root of each pack and has none; some node has exactly 3. `lengths`: the used tokens are the first ones of the tile; the root's tile is full.
All inputs are finite; a program needn't handle non-finite values.
Results may differ from the reference program's by a relative error of at most 0.023.
Values may be sent and summed in bfloat16 or wider, within the bound.
No kernel may reach another device: no remote copies, remote signals or barrier semaphores. Data moves between devices by JAX's collectives and lax.ppermute only.
A program may use at most 128 MiB of HBM per device.

```python
import math
import jax
import jax.numpy as jnp
from jax import lax

HD = 128
QH = 4
DW = 4096
TILE = 512
ANC = 3
NODE_DEV = 1
QW = 512
NODES = 32
PACKS = 8
N_SEQ = 32


def draw_queries(key, part):
    key = jax.random.fold_in(key, 3)
    drawn = jnp.clip(jax.random.normal(key, (PACKS, NODES, TILE, QW), jnp.float32), -6.0, 6.0)
    return drawn.astype(jnp.bfloat16)


def draw_keys(key, part):
    key = jax.random.fold_in(key, 5)
    drawn = jnp.clip(jax.random.normal(key, (PACKS, NODES, TILE, HD), jnp.float32), -6.0, 6.0)
    return drawn.astype(jnp.bfloat16)


def draw_lengths(key, part):
    key = jax.random.fold_in(key, 9)
    drawn = jax.random.randint(key, (PACKS, NODES), TILE // 4, TILE + 1, dtype=jnp.int32)
    first_column = lax.broadcasted_iota(jnp.int32, (PACKS, NODES), 1) == 0
    return jnp.where(first_column, TILE, drawn).astype(jnp.int32)


def draw_ancestors(key, part):
    key = jax.random.fold_in(key, 7)
    picks = jax.random.randint(key, (PACKS, NODES), 0, 1 << 20, dtype=jnp.int32)
    column = jnp.arange(ANC, dtype=jnp.int32)

    def one_pack(pick_row):

        def grow(table, node):
            chosen = pick_row[node] % jnp.maximum(node, 1)
            parent = jnp.where(node <= ANC, node - 1, chosen)
            parent = jnp.where(node == NODES - 2, 0, parent)
            parent = jnp.where(node == NODES - 1, NODES - 2, parent)
            parent = jnp.maximum(parent, 0).astype(jnp.int32)
            above = table[parent]
            level = jnp.sum((above >= 0).astype(jnp.int32))
            parent = jnp.where(level >= ANC, above[ANC - 1], parent).astype(jnp.int32)
            above = table[parent]
            level = jnp.sum((above >= 0).astype(jnp.int32))
            row_new = jnp.where(column == level, parent, above)
            row_new = jnp.where(node == 0, -1, row_new).astype(jnp.int32)
            return (table.at[node].set(row_new), None)
        start_table = jnp.full((NODES, ANC), -1, jnp.int32)
        table, _ = lax.scan(grow, start_table, jnp.arange(NODES, dtype=jnp.int32))
        return table
    return jax.vmap(one_pack)(picks)


def levels(key, shape, cuts, smallest, top_value):
    def one(position, parts):
        steps = jax.random.uniform(jax.random.fold_in(jax.random.fold_in(key, 6), position), (parts,), jnp.float32, smallest / len(cuts), top_value / len(cuts))
        return jnp.repeat(jnp.exp(steps), shape[position] // parts).reshape((-1,) + (1,) * (len(shape) - position - 1))

    loudness = one(*cuts[0])
    for cut in cuts[1:]:
        loudness = loudness * one(*cut)
    return loudness


def gaussian(rng, shape, spread, limit, shards=(), held_as=jnp.bfloat16):
    factor_of = levels(rng, shape, shards, -0.22, 0.18) if shards else 1.0
    values = jax.random.normal(rng, shape, jnp.float32) * spread * factor_of
    return jnp.minimum(jnp.maximum(values, -limit), limit).astype(held_as)


def setup_inputs(seed: int = 0) -> dict:
    streams_of = jax.random.split(jax.random.key(seed), 9)
    return {
        "queries": draw_queries(jax.random.fold_in(streams_of[8], 71), 0),
        "keys": draw_keys(jax.random.fold_in(streams_of[8], 71), 0),
        "values": gaussian(streams_of[2], (PACKS, NODES, TILE, HD), 1.0, 6.0, ((0, 8), (1, 32))),
        "grad_out": gaussian(streams_of[3], (PACKS, NODES, TILE, DW), 1.0, 6.0, ((0, 8), (1, 32))),
        "out_weight": gaussian(streams_of[4], (DW, QW), QW ** -0.5, 0.25, ((0, 8),)),
        "ancestors": draw_ancestors(jax.random.fold_in(streams_of[8], 71), 0),
        "owner": jax.vmap(lambda own: jax.random.permutation(own, NODES))(jax.random.split(streams_of[6], PACKS)).reshape((PACKS, NODES)).astype(jnp.int32),
        "lengths": draw_lengths(jax.random.fold_in(streams_of[8], 71), 0),
    }


MASKED = -1e+30

def slot_tables(ancestor_table, owner_row, length_row):
    node_count = owner_row.shape[0]
    node_ids = jnp.arange(node_count, dtype=jnp.int32)
    matches = owner_row[:, None] == node_ids[None, :]
    node_of_slot = lax.optimization_barrier(jnp.sum(jnp.where(matches, node_ids[:, None], 0), axis=0)).astype(jnp.int32)
    tile_length = lax.optimization_barrier(jnp.sum(jnp.where(matches, length_row[:, None], 0), axis=0)).astype(jnp.int32)
    ancestor_nodes = lax.optimization_barrier(jnp.sum(jnp.where(matches[:, :, None], ancestor_table[:, None, :], 0), axis=0)).astype(jnp.int32)
    ancestor_hits = ancestor_nodes[:, :, None] == node_ids[None, None, :]
    ancestor_slots = lax.optimization_barrier(jnp.sum(jnp.where(ancestor_hits, owner_row[None, None, :], 0), axis=2)).astype(jnp.int32)
    ancestor_slots = jnp.where(ancestor_nodes >= 0, ancestor_slots, -1).astype(jnp.int32)
    key_slots = jnp.concatenate([ancestor_slots, node_ids[:, None]], axis=1).astype(jnp.int32)
    return (key_slots, tile_length)

def key_visible(key_length, self_tile, tile_size):
    query_pos = lax.broadcasted_iota(jnp.int32, (tile_size, tile_size), 0)
    key_pos = lax.broadcasted_iota(jnp.int32, (tile_size, tile_size), 1)
    return (key_pos < key_length) & ((key_pos <= query_pos) | jnp.logical_not(self_tile))

def tile_terms(tile_index, pack_queries, pack_keys, pack_values, grad_attn_all, key_slots, tile_length):
    score_scale = 1.0 / math.sqrt(HD)
    tile_query = pack_queries[tile_index].astype(jnp.float32).reshape(TILE, QH, HD)
    grad_attn = grad_attn_all[tile_index].astype(jnp.float32)
    tile_slots = key_slots[tile_index]
    step_order = jnp.arange(ANC + 1, dtype=jnp.int32)

    def logits(step_index):
        safe_slot = jnp.maximum(tile_slots[step_index], 0)
        key_part = pack_keys[safe_slot].astype(jnp.float32)
        value_part = pack_values[safe_slot].astype(jnp.float32)
        visible = key_visible(tile_length[safe_slot], step_index == ANC, TILE)
        scores = jnp.einsum('qhd,kd->qhk', tile_query, key_part) * score_scale
        return (jnp.where(visible[:, None, :], scores, MASKED), visible, key_part, value_part, safe_slot)

    def forward(carried, step_index):

        def take_tile(forward_state):
            row_max, row_total, weighted = forward_state
            scores, visible, key_part, value_part, safe_slot = logits(step_index)
            new_max = jnp.maximum(row_max, lax.optimization_barrier(jnp.max(scores, axis=2)))
            weights = jnp.where(visible[:, None, :], jnp.exp(scores - new_max[..., None]), 0.0)
            factor = jnp.exp(row_max - new_max)
            weights_low = lax.optimization_barrier(weights.astype(jnp.bfloat16)).astype(jnp.float32)
            product = jnp.einsum('qhk,kd->qhd', weights_low, value_part)
            return (new_max, row_total * factor + lax.optimization_barrier(jnp.sum(weights, axis=2)), weighted * factor[..., None] + product)
        return (lax.cond(tile_slots[step_index] >= 0, take_tile, lambda forward_state: forward_state, carried), None)
    initial = (jnp.full((TILE, QH), MASKED, jnp.float32), jnp.zeros((TILE, QH), jnp.float32), jnp.zeros((TILE, QH, HD), jnp.float32))
    (row_max, row_total, weighted), _ = lax.scan(forward, initial, step_order)
    attention = weighted / row_total[..., None]
    log_total = row_max + jnp.log(row_total)
    row_delta = lax.optimization_barrier(jnp.sum(grad_attn * attention, axis=-1))

    def backward(grad_query, step_index):

        def take_tile(back_state):
            scores, visible, key_part, value_part, safe_slot = logits(step_index)
            probabilities = jnp.where(visible[:, None, :], jnp.exp(scores - log_total[..., None]), 0.0)
            probs_low = lax.optimization_barrier(probabilities.astype(jnp.bfloat16)).astype(jnp.float32)
            grad_probs = jnp.einsum('qhd,kd->qhk', grad_attn, value_part)
            grad_scores = probabilities * (grad_probs - row_delta[..., None]) * score_scale
            grad_scores = lax.optimization_barrier(grad_scores.astype(jnp.bfloat16)).astype(jnp.float32)
            new_query = back_state + jnp.einsum('qhk,kd->qhd', grad_scores, key_part)
            grad_key_part = jnp.einsum('qhk,qhd->kd', grad_scores, tile_query)
            grad_value_part = jnp.einsum('qhk,qhd->kd', probs_low, grad_attn)
            return (new_query, jnp.concatenate([grad_key_part, grad_value_part], axis=-1))

        def skip_tile(back_state):
            return (back_state, jnp.zeros((TILE, 2 * HD), jnp.float32))
        return lax.cond(tile_slots[step_index] >= 0, take_tile, skip_tile, grad_query)
    grad_query, key_parts = lax.scan(backward, jnp.zeros((TILE, QH, HD), jnp.float32), step_order)
    return (attention.reshape(TILE, QW).astype(jnp.bfloat16), grad_query.reshape(TILE, QW).astype(jnp.bfloat16), key_parts)

def reference(queries, keys, values, grad_out, out_weight, ancestors, owner, lengths):

    def one_pack(weight_total, pack_inputs):
        pack_queries, pack_keys, pack_values, pack_grads, ancestor_table, owner_row, length_row = pack_inputs
        key_slots, tile_length = slot_tables(ancestor_table, owner_row, length_row)
        positions = lax.broadcasted_iota(jnp.int32, (NODES, TILE), 1)
        masked_grads = jnp.where((positions < tile_length[:, None])[..., None], pack_grads, jnp.zeros((), jnp.bfloat16))
        flat_grads = masked_grads.reshape(NODES * TILE, DW)
        grad_attn_all = jnp.dot(flat_grads, out_weight, preferred_element_type=jnp.float32).astype(jnp.bfloat16)
        grad_attn_all = grad_attn_all.reshape(NODES, TILE, QH, HD)

        def per_query(tile_index):
            return tile_terms(tile_index, pack_queries, pack_keys, pack_values, grad_attn_all, key_slots, tile_length)
        attention_low, grad_query, key_parts = lax.map(per_query, jnp.arange(NODES, dtype=jnp.int32))
        targets = jnp.maximum(key_slots, 0).astype(jnp.int32)

        def per_device(key_total, device_index):
            device_rows = lax.dynamic_slice_in_dim(key_parts, device_index * NODE_DEV, NODE_DEV, 0)
            device_aims = lax.dynamic_slice_in_dim(targets, device_index * NODE_DEV, NODE_DEV, 0)
            partial_sum = jnp.zeros((NODES, TILE, 2 * HD), jnp.float32).at[device_aims.reshape(-1)].add(device_rows.reshape(-1, TILE, 2 * HD))
            return (key_total + lax.optimization_barrier(partial_sum.astype(jnp.bfloat16)).astype(jnp.float32), None)
        key_total, _ = lax.scan(per_device, jnp.zeros((NODES, TILE, 2 * HD), jnp.float32), jnp.arange(N_SEQ, dtype=jnp.int32))
        weight_total = weight_total + jnp.dot(flat_grads.T, attention_low.reshape(NODES * TILE, QW), preferred_element_type=jnp.float32)
        grad_key_out = key_total[..., :HD].astype(jnp.bfloat16)
        grad_value_out = key_total[..., HD:].astype(jnp.bfloat16)
        return (weight_total, (grad_query, grad_key_out, grad_value_out))
    pack_inputs = (queries, keys, values, grad_out, ancestors, owner, lengths)
    weight_total, (grad_queries, grad_keys, grad_values) = lax.scan(one_pack, jnp.zeros((DW, QW), jnp.float32), pack_inputs)
    grad_weight = weight_total / math.sqrt(PACKS * NODES * TILE)
    return (grad_queries, grad_keys, grad_values, grad_weight)
```

```python
import math

import jax
import jax.numpy as jnp
from jax import lax
from jax.experimental import pallas as pl
from jax.experimental.pallas import tpu as pltpu
from jax.sharding import Mesh, PartitionSpec as P

BF = jnp.bfloat16
F32 = jnp.float32
MASKED = -1e30
LOG2E = 1.0 / math.log(2.0)
VMEM_LIMIT = 48 * 1024 * 1024
SMEM_SPEC = pl.BlockSpec(memory_space=pltpu.SMEM)
VMEM_SPEC = pl.BlockSpec(memory_space=pltpu.VMEM)
ROWS = 256


def nn(a, b):
    return lax.dot_general(a, b, (((1,), (0,)), ((), ())), preferred_element_type=F32)


def tn(a, b):
    return lax.dot_general(a, b, (((0,), (0,)), ((), ())), preferred_element_type=F32)


def params():
    return pltpu.CompilerParams(vmem_limit_bytes=VMEM_LIMIT)


def route_kernel(me_ref, anc_ref, owner_ref, len_ref, chunk_ref, out_ref, info_ref):
    nodes, depth = anc_ref.shape
    me = me_ref[0]

    def one_node(n, carry):
        slot = owner_ref[n]
        mine = slot == me

        @pl.when(mine)
        def _():
            info_ref[depth] = len_ref[n]

        for k in range(depth):
            a = anc_ref[n, k]
            present = a >= 0
            safe = jnp.maximum(a, 0)
            source = owner_ref[safe]

            @pl.when(present)
            def _():
                out_ref[slot, k] = chunk_ref[source]

            @pl.when(jnp.logical_not(present))
            def _():
                out_ref[slot, k] = jnp.zeros(out_ref.shape[2:], out_ref.dtype)

            @pl.when(mine)
            def _():
                info_ref[k] = jnp.where(present, len_ref[safe], 0)

        return carry

    lax.fori_loop(0, nodes, one_node, 0)


def route(me, anc, owner, lengths, chunks):
    nodes, depth = anc.shape
    return pl.pallas_call(
        route_kernel,
        out_shape=(
            jax.ShapeDtypeStruct((nodes, depth) + chunks.shape[1:], BF),
            jax.ShapeDtypeStruct((depth + 1,), jnp.int32),
        ),
        in_specs=[SMEM_SPEC] * 4 + [VMEM_SPEC],
        out_specs=(VMEM_SPEC, SMEM_SPEC),
        compiler_params=params(),
        name="route",
    )(me, anc, owner, lengths, chunks)


def load_tiles(self_ref, anc_ref, kt_ref, vt_ref, k_ref=None, v_ref=None):
    head = kt_ref.shape[0]
    tile = self_ref.shape[0]
    depth = anc_ref.shape[1]
    for j in range(depth + 1):
        if j < depth:
            kv = anc_ref[:, j].reshape(tile, 2 * head)
        else:
            kv = self_ref[...]
        k_part, v_part = kv[:, :head], kv[:, head:]
        at = slice(j * tile, (j + 1) * tile)
        kt_ref[:, at] = k_part.T
        if vt_ref is not None:
            vt_ref[:, at] = v_part.T
        if k_ref is not None:
            k_ref[at] = k_part
        if v_ref is not None:
            v_ref[at] = v_part


def fill_bias(info_ref, bias_ref, tile):
    tiles = bias_ref.shape[1] // tile
    pos = lax.broadcasted_iota(jnp.int32, (1, tile), 1)
    for j in range(tiles):
        bias_ref[:, j * tile : (j + 1) * tile] = jnp.where(pos < info_ref[j], 0.0, MASKED)


def block_logits(q, kt_ref, bias_ref, first, width, tile, scale):
    s = nn(q, kt_ref[:, :width]) * scale + bias_ref[:, :width]
    base = kt_ref.shape[1] - tile + first
    q_pos = lax.broadcasted_iota(jnp.int32, (ROWS, ROWS), 0)
    k_pos = lax.broadcasted_iota(jnp.int32, (ROWS, ROWS), 1)
    diagonal = jnp.where(k_pos <= q_pos, s[:, base : base + ROWS], MASKED)
    return jnp.concatenate([s[:, :base], diagonal], axis=1)


def forward_kernel(info_ref, q_ref, g_ref, self_ref, anc_ref, att_ref, stat_ref, kt_ref, v_ref, bias_ref):
    tile, width = q_ref.shape
    head = kt_ref.shape[0]
    heads = width // head
    depth = anc_ref.shape[1]
    length = info_ref[depth]
    load_tiles(self_ref, anc_ref, kt_ref, None, None, v_ref)
    fill_bias(info_ref, bias_ref, tile)
    scale = LOG2E / math.sqrt(head)
    for first in range(0, tile, ROWS):
        at = slice(first, first + ROWS)
        keys = depth * tile + first + ROWS
        row_ok = first + lax.broadcasted_iota(jnp.int32, (ROWS, 1), 0) < length
        for h in range(heads):
            cols = slice(h * head, (h + 1) * head)
            s = block_logits(q_ref[at, cols], kt_ref, bias_ref, first, keys, tile, scale)
            top = jnp.max(s, axis=1, keepdims=True)
            w = jnp.exp2(s - top)
            total = jnp.sum(w, axis=1, keepdims=True)
            att = nn(w.astype(BF), v_ref[:keys]) / total
            g = jnp.where(row_ok, g_ref[at, cols], jnp.zeros((), BF)).astype(F32)
            stat_ref[at, h : h + 1] = top + jnp.log2(total)
            stat_ref[at, heads + h : heads + h + 1] = jnp.sum(g * att, axis=1, keepdims=True)
            att_ref[at, cols] = jnp.where(row_ok, att, 0.0).astype(BF)


def forward(info, q, g, kv_self, kv_anc):
    tile, width = q.shape
    head = kv_self.shape[1] // 2
    keys = (kv_anc.shape[1] + 1) * tile
    return pl.pallas_call(
        forward_kernel,
        out_shape=(
            jax.ShapeDtypeStruct((tile, width), BF),
            jax.ShapeDtypeStruct((tile, 2 * (width // head)), F32),
        ),
        in_specs=[SMEM_SPEC] + [VMEM_SPEC] * 4,
        out_specs=(VMEM_SPEC, VMEM_SPEC),
        scratch_shapes=[
            pltpu.VMEM((head, keys), BF),
            pltpu.VMEM((keys, head), BF),
            pltpu.VMEM((1, keys), F32),
        ],
        compiler_params=params(),
        name="forward",
    )(info, q, g, kv_self, kv_anc)


def backward_kernel(
    info_ref, q_ref, g_ref, stat_ref, self_ref, anc_ref,
    dq_ref, term_ref, own_ref,
    kt_ref, vt_ref, k_ref, bias_ref, dk_ref, dv_ref,
):
    tile, width = q_ref.shape
    head = kt_ref.shape[0]
    heads = width // head
    depth = anc_ref.shape[1]
    length = info_ref[depth]
    load_tiles(self_ref, anc_ref, kt_ref, vt_ref, k_ref)
    fill_bias(info_ref, bias_ref, tile)
    root = 1.0 / math.sqrt(head)
    scale = LOG2E * root
    dk_ref[...] = jnp.zeros_like(dk_ref)
    dv_ref[...] = jnp.zeros_like(dv_ref)
    for first in range(0, tile, ROWS):
        at = slice(first, first + ROWS)
        keys = depth * tile + first + ROWS
        row_ok = first + lax.broadcasted_iota(jnp.int32, (ROWS, 1), 0) < length
        for h in range(heads):
            cols = slice(h * head, (h + 1) * head)
            q = q_ref[at, cols]
            g = jnp.where(row_ok, g_ref[at, cols], jnp.zeros((), BF))
            s = block_logits(q, kt_ref, bias_ref, first, keys, tile, scale)
            p = jnp.exp2(s - stat_ref[at, h : h + 1])
            dp = nn(g, vt_ref[:, :keys])
            ds = (p * (dp - stat_ref[at, heads + h : heads + h + 1])).astype(BF)
            p = p.astype(BF)
            dq_ref[at, cols] = (nn(ds, k_ref[:keys]) * root).astype(BF)
            dk_ref[:keys] += tn(ds, q)
            dv_ref[:keys] += tn(p, g)
    for j in range(depth):
        rows = slice(j * tile, (j + 1) * tile)
        shape = (tile // 16, 16, head)
        term_ref[:, j, :, :head] = (dk_ref[rows] * root).astype(BF).reshape(shape)
        term_ref[:, j, :, head:] = dv_ref[rows].astype(BF).reshape(shape)
    own_ref[:, :head] = dk_ref[depth * tile :] * root
    own_ref[:, head:] = dv_ref[depth * tile :]


def backward(info, q, g, stat, kv_self, kv_anc):
    tile, width = q.shape
    head = kv_self.shape[1] // 2
    keys = (kv_anc.shape[1] + 1) * tile
    return pl.pallas_call(
        backward_kernel,
        out_shape=(
            jax.ShapeDtypeStruct((tile, width), BF),
            jax.ShapeDtypeStruct(kv_anc.shape, BF),
            jax.ShapeDtypeStruct((tile, 2 * head), F32),
        ),
        in_specs=[SMEM_SPEC] + [VMEM_SPEC] * 5,
        out_specs=(VMEM_SPEC,) * 3,
        scratch_shapes=[
            pltpu.VMEM((head, keys), BF),
            pltpu.VMEM((head, keys), BF),
            pltpu.VMEM((keys, head), BF),
            pltpu.VMEM((1, keys), F32),
            pltpu.VMEM((keys, head), F32),
            pltpu.VMEM((keys, head), F32),
        ],
        compiler_params=params(),
        name="backward",
    )(info, q, g, stat, kv_self, kv_anc)


def collect_kernel(anc_ref, owner_ref, term_ref, *refs):
    part_refs, (out_ref, sum_ref) = refs[:-2], refs[-2:]
    nodes, depth = anc_ref.shape
    width = term_ref.shape[3]
    sum_ref[...] = jnp.zeros_like(sum_ref)

    def one_node(n, carry):
        slot = owner_ref[n]
        for k in range(depth):
            a = anc_ref[n, k]

            @pl.when(a >= 0)
            def _():
                target = owner_ref[jnp.maximum(a, 0)]
                sum_ref[target] += term_ref[slot, k].astype(F32)

        return carry

    lax.fori_loop(0, nodes, one_node, 0)
    out_ref[:, :, :width] = sum_ref[...].astype(BF)
    total = part_refs[0][...].astype(F32)
    for part in part_refs[1:]:
        total = total + part[...].astype(F32)
    out_ref[:, :, width:] = total.astype(BF).reshape(out_ref.shape[0], 16, -1)


def collect(anc, owner, terms, parts):
    nodes = anc.shape[0]
    width = terms.shape[3]
    return pl.pallas_call(
        collect_kernel,
        out_shape=jax.ShapeDtypeStruct((nodes, 16, width + parts[0].shape[1]), BF),
        in_specs=[SMEM_SPEC] * 2 + [VMEM_SPEC] * (1 + len(parts)),
        out_specs=VMEM_SPEC,
        scratch_shapes=[pltpu.VMEM((nodes, 16, width), F32)],
        compiler_params=params(),
        name="collect",
    )(anc, owner, terms, *parts)


def finish_kernel(weight_scale, got_ref, own_ref, gk_ref, gv_ref, gw_ref):
    tile, width = own_ref.shape
    head = width // 2
    total = got_ref[:, :, :width].reshape(tile, width).astype(F32) + own_ref[...]
    gk_ref[...] = total[:, :head].astype(BF)
    gv_ref[...] = total[:, head:].astype(BF)
    gw_ref[...] = jnp.sum(got_ref[:, :, width:].astype(F32), axis=0) * weight_scale


def finish(got, own, weight_scale):
    tile, width = own.shape
    return pl.pallas_call(
        lambda *refs: finish_kernel(weight_scale, *refs),
        out_shape=(
            jax.ShapeDtypeStruct((tile, width // 2), BF),
            jax.ShapeDtypeStruct((tile, width // 2), BF),
            jax.ShapeDtypeStruct((16, got.shape[2] - width), F32),
        ),
        in_specs=[VMEM_SPEC] * 2,
        out_specs=(VMEM_SPEC,) * 3,
        compiler_params=params(),
        name="finish",
    )(got, own)


def ring(size, step):
    return [(i, (i + step) % size) for i in range(size)]


def per_device(queries, keys, values, grad_out, out_weight, ancestors, owner, lengths):
    q = queries[0, 0]
    tile, width = q.shape
    head = keys.shape[-1]
    seq = ("z", "y")
    nodes = lax.axis_size(seq)
    xs = lax.axis_size("x")
    core = lax.axis_index("core")
    x = lax.axis_index("x")
    me = lax.axis_index(seq).astype(jnp.int32).reshape(1)
    anc, own_row, len_row = ancestors[0], owner[0], lengths[0]

    weight = lax.all_gather(out_weight, ("x", "core"), axis=0, tiled=True)
    grads = grad_out[0, 0]
    block = grads.shape[1] // (2 * xs)
    halves = grads.reshape(tile, xs, 2, block)
    mine = lax.dynamic_index_in_dim(halves, core, 2, keepdims=False).reshape(tile, xs * block)
    other = lax.dynamic_index_in_dim(halves, 1 - core, 2, keepdims=False).reshape(tile, xs * block)
    sibling = lax.ppermute(other, "core", ring(2, 1))

    kv_self = jnp.concatenate([keys[0, 0], values[0, 0]], axis=-1)
    chunks = lax.all_to_all(kv_self.reshape(nodes, 16, 2 * head), seq, 0, 0, tiled=True)
    routed, info = route(me, anc, own_row, len_row, chunks)
    kv_anc = lax.all_to_all(routed, seq, 0, 0, tiled=True)

    grad_att = jnp.dot(grads, weight, preferred_element_type=F32).astype(BF)
    att, stat = forward(info, q, grad_att, kv_self, kv_anc)

    att_sibling = lax.ppermute(att, "core", ring(2, 1))
    both_grads = jnp.concatenate([mine, sibling], axis=0)
    both_att = jnp.concatenate([att, att_sibling], axis=0)
    product = tn(both_grads, both_att).astype(BF).reshape(xs, block, width)
    parts = [lax.dynamic_index_in_dim(product, x, 0, keepdims=False)]
    for step in range(1, xs):
        piece = lax.dynamic_index_in_dim(product, (x + step) % xs, 0, keepdims=False)
        parts.append(lax.ppermute(piece, "x", ring(xs, step)))

    grad_q, terms, own = backward(info, q, grad_att, stat, kv_self, kv_anc)
    terms = lax.all_to_all(terms, seq, 0, 0, tiled=True)
    summed = collect(anc, own_row, terms, parts)
    got = lax.all_to_all(summed, seq, 0, 0, tiled=True)
    token_count = 2 * xs * nodes * tile
    grad_k, grad_v, grad_w = finish(got, own, 1.0 / math.sqrt(token_count))
    return grad_q[None, None], grad_k[None, None], grad_v[None, None], grad_w


def solution(mesh):
    dp, seq = mesh.devices.shape
    fine = Mesh(mesh.devices.reshape(dp // 2, 2, seq // 4, 4), ("x", "core", "z", "y"))
    d, s = ("x", "core"), ("z", "y")
    placed = (
        P(d, s, None, None),
        P(d, s, None, None),
        P(d, s, None, None),
        P(d, s, None, None),
        P(d, None),
        P(d, None, None),
        P(d, None),
        P(d, None),
    )
    return jax.shard_map(
        per_device,
        mesh=fine,
        in_specs=placed,
        out_specs=(
            P(d, s, None, None),
            P(d, s, None, None),
            P(d, s, None, None),
            P(d + s, None),
        ),
        check_vma=False,
    )
```

```python
import math

import jax
import jax.numpy as jnp
from jax import lax
from jax.experimental import pallas as pl
from jax.experimental.pallas import tpu as pltpu
from jax.sharding import Mesh, PartitionSpec as P

BF = jnp.bfloat16
F32 = jnp.float32
MASKED = -1e30
LOG2E = 1.0 / math.log(2.0)
MIB = 1024 * 1024
VMEM_MIB = 8
SMEM_SPEC = pl.BlockSpec(memory_space=pltpu.SMEM)
VMEM_SPEC = pl.BlockSpec(memory_space=pltpu.VMEM)
ROWS = 256


def nn(a, b):
    return lax.dot_general(a, b, (((1,), (0,)), ((), ())), preferred_element_type=F32)


def tn(a, b):
    return lax.dot_general(a, b, (((0,), (0,)), ((), ())), preferred_element_type=F32)


def params(mib=VMEM_MIB):
    return pltpu.CompilerParams(vmem_limit_bytes=mib * MIB)


def cost(flops, moved):
    return pl.CostEstimate(flops=int(flops), bytes_accessed=int(moved), transcendentals=0)


def long_cost():
    return cost(10**13, 10**11)


def join_kernel(k_ref, v_ref, out_ref):
    head = k_ref.shape[2]
    out_ref[:, :, :head] = k_ref[...]
    out_ref[:, :, head:] = v_ref[...]


def join(k, v):
    tile, head = k.shape
    shape = (tile // 16, 16, head)
    return pl.pallas_call(
        join_kernel,
        out_shape=jax.ShapeDtypeStruct((tile // 16, 16, 2 * head), BF),
        in_specs=[VMEM_SPEC] * 2,
        out_specs=VMEM_SPEC,
        compiler_params=params(56),
        cost_estimate=cost(0, 8 * k.size),
        name="join",
    )(k.reshape(shape), v.reshape(shape))


def halves_kernel(place_ref, in_ref, out_ref):
    out_ref[...] = in_ref[...]


def other_half(place, grads, xs):
    tile, features = grads.shape
    block = features // (2 * xs)
    return pl.pallas_call(
        halves_kernel,
        grid_spec=pltpu.PrefetchScalarGridSpec(
            num_scalar_prefetch=1,
            grid=(xs,),
            in_specs=[pl.BlockSpec((tile, block), lambda i, place: (0, 2 * i + 1 - place[1]))],
            out_specs=pl.BlockSpec((tile, block), lambda i, place: (0, i)),
        ),
        out_shape=jax.ShapeDtypeStruct((tile, features // 2), BF),
        compiler_params=params(),
        cost_estimate=long_cost(),
        name="other_half",
    )(place, grads)


def grad_attention_kernel(runs, place_ref, grads_ref, *refs):
    refs, (out_ref, sum_ref) = list(refs[:-2]), refs[-2:]
    step = pl.program_id(0)
    for i, count in enumerate(runs):
        block, refs = refs[:count], refs[count:]

        @pl.when(step == i)
        def _():
            product, first = 0.0, 0
            for rows in block:
                last = first + rows.shape[0]
                product, first = product + nn(grads_ref[:, first:last], rows[...]), last
            if i == 0:
                sum_ref[...] = product
            elif i < len(runs) - 1:
                sum_ref[...] += product
            else:
                out_ref[...] = (sum_ref[...] + product).astype(BF)


def grad_attention(place, xs, grads, blocks):
    tile, features = grads.shape
    runs = [rows for block in blocks for rows in block]
    width = runs[0].shape[1]
    block = features // (2 * xs)

    def column(i, place):
        source = lax.rem(place[0] + xs - lax.div(i, 2), xs)
        return 0, 2 * source + lax.rem(place[1] + i, 2)

    return pl.pallas_call(
        lambda *refs: grad_attention_kernel([len(block) for block in blocks], *refs),
        grid_spec=pltpu.PrefetchScalarGridSpec(
            num_scalar_prefetch=1,
            grid=(2 * xs,),
            in_specs=[pl.BlockSpec((tile, block), column)]
            + [pl.BlockSpec(rows.shape, lambda i, place: (0, 0)) for rows in runs],
            out_specs=pl.BlockSpec((tile, width), lambda i, place: (0, 0)),
            scratch_shapes=[pltpu.VMEM((tile, width), F32)],
        ),
        out_shape=jax.ShapeDtypeStruct((tile, width), BF),
        compiler_params=params(16),
        cost_estimate=cost(2 * tile * features * width, 2 * (tile + width) * features),
        name="grad_attention",
    )(place, grads, *runs)


def pieces_kernel(place_ref, mine_ref, sibling_ref, att_ref, att_sibling_ref, *refs):
    out_refs, (mine_t_ref, sibling_t_ref) = refs[:-2], refs[-2:]

    @pl.when(pl.program_id(0) == 0)
    def _():
        mine_t_ref[...] = att_ref[...].T
        sibling_t_ref[...] = att_sibling_ref[...].T

    total = nn(mine_t_ref[...], mine_ref[...]) + nn(sibling_t_ref[...], sibling_ref[...])
    total = total.astype(BF)
    for k, out_ref in enumerate(out_refs):

        @pl.when(pl.program_id(0) == k)
        def _():
            out_ref[...] = total


def make_pieces(place, xs, grads, sibling, att, att_sibling):
    tile, features = grads.shape
    block = features // (2 * xs)
    width = att.shape[1]
    whole = pl.BlockSpec((tile, width), lambda i, place: (0, 0))
    return pl.pallas_call(
        pieces_kernel,
        grid_spec=pltpu.PrefetchScalarGridSpec(
            num_scalar_prefetch=1,
            grid=(xs,),
            in_specs=[
                pl.BlockSpec(
                    (tile, block),
                    lambda i, place: (0, 2 * lax.rem(place[0] + i, xs) + place[1]),
                ),
                pl.BlockSpec((tile, block), lambda i, place: (0, lax.rem(place[0] + i, xs))),
                whole,
                whole,
            ],
            out_specs=(pl.BlockSpec((width, block), lambda i, place: (0, 0)),) * xs,
            scratch_shapes=[pltpu.VMEM((width, tile), BF)] * 2,
        ),
        out_shape=(jax.ShapeDtypeStruct((width, block), BF),) * xs,
        compiler_params=params(16),
        cost_estimate=cost(4 * tile * block * width * xs, 2 * xs * (2 * tile * block + block * width)),
        name="pieces",
    )(place, grads, sibling, att, att_sibling)


def join_tables(anc, owner, lengths, me):
    return jnp.concatenate([anc.reshape(-1), owner, lengths, me])


def route_kernel(table_ref, chunk_ref, out_ref, info_ref):
    nodes, depth = out_ref.shape[:2]
    owner, lengths = nodes * depth, nodes * (depth + 1)
    me = table_ref[nodes * (depth + 2)]
    zero = jnp.zeros(out_ref.shape[2:], out_ref.dtype)

    def one_node(n, mine):
        slot = table_ref[owner + n]
        for k in range(depth):
            a = table_ref[n * depth + k]
            source = table_ref[owner + jnp.maximum(a, 0)]
            out_ref[slot, k] = jnp.where(a >= 0, chunk_ref[source], zero)
        return jnp.where(slot == me, n, mine)

    mine = lax.fori_loop(0, nodes, one_node, 0, unroll=4)
    for k in range(depth):
        a = table_ref[mine * depth + k]
        info_ref[k] = jnp.where(a >= 0, table_ref[lengths + jnp.maximum(a, 0)], 0)
    info_ref[depth] = table_ref[lengths + mine]


def route(table, chunks, depth):
    nodes = chunks.shape[0]
    return pl.pallas_call(
        route_kernel,
        out_shape=(
            jax.ShapeDtypeStruct((nodes, depth) + chunks.shape[1:], BF),
            jax.ShapeDtypeStruct((depth + 1,), jnp.int32),
        ),
        in_specs=[SMEM_SPEC, VMEM_SPEC],
        out_specs=(VMEM_SPEC, SMEM_SPEC),
        compiler_params=params(),
        cost_estimate=cost(0, 8 * depth * chunks.size),
        name="route",
    )(table, chunks)


def load_tiles(self_ref, anc_ref, kt_ref, vt_ref, k_ref=None, v_ref=None):
    head = kt_ref.shape[0]
    depth = anc_ref.shape[1]
    tile = anc_ref.shape[0] * anc_ref.shape[2]
    for j in range(kt_ref.shape[1] // tile):
        if j < depth:
            kv = anc_ref[:, j].reshape(tile, 2 * head)
        else:
            kv = self_ref[...].reshape(tile, 2 * head)
        k_part, v_part = kv[:, :head], kv[:, head:]
        at = slice(j * tile, (j + 1) * tile)
        kt_ref[:, at] = k_part.T
        if vt_ref is not None:
            vt_ref[:, at] = v_part.T
        if k_ref is not None:
            k_ref[at] = k_part
        if v_ref is not None:
            v_ref[at] = v_part


def fill_bias(info_ref, bias_ref, tile):
    tiles = bias_ref.shape[1] // tile
    pos = lax.broadcasted_iota(jnp.int32, (1, tile), 1)
    for j in range(tiles):
        bias_ref[:, j * tile : (j + 1) * tile] = jnp.where(pos < info_ref[j], 0.0, MASKED)


def block_logits(q, kt_ref, bias_ref, first, width, tile, scale):
    s = nn(q, kt_ref[:, :width]) * scale + bias_ref[:, :width]
    base = kt_ref.shape[1] - tile + first
    q_pos = lax.broadcasted_iota(jnp.int32, (ROWS, ROWS), 0)
    k_pos = lax.broadcasted_iota(jnp.int32, (ROWS, ROWS), 1)
    diagonal = jnp.where(k_pos <= q_pos, s[:, base : base + ROWS], MASKED)
    return jnp.concatenate([s[:, :base], diagonal], axis=1)


def forward_kernel(
    info_ref, q_ref, self_ref, anc_ref, att_ref, low_ref, log_ref, kt_ref, v_ref, bias_ref
):
    tile, width = q_ref.shape
    head = kt_ref.shape[0]
    depth = anc_ref.shape[1]
    length = info_ref[depth]
    load_tiles(self_ref, anc_ref, kt_ref, None, None, v_ref)
    fill_bias(info_ref, bias_ref, tile)
    scale = LOG2E / math.sqrt(head)
    for first in range(0, tile, ROWS):
        at = slice(first, first + ROWS)
        keys = depth * tile + first + ROWS
        row_ok = first + lax.broadcasted_iota(jnp.int32, (ROWS, 1), 0) < length
        for h in range(width // head):
            cols = slice(h * head, (h + 1) * head)
            s = block_logits(q_ref[at, cols], kt_ref, bias_ref, first, keys, tile, scale)
            top = jnp.max(s, axis=1, keepdims=True)
            w = jnp.exp2(s - top)
            total = jnp.sum(w, axis=1, keepdims=True)
            att = nn(w.astype(BF), v_ref[:keys]) / total
            log_ref[at, h : h + 1] = top + jnp.log2(total)
            att_ref[at, cols] = att
            low_ref[at, cols] = jnp.where(row_ok, att, 0.0).astype(BF)


def forward(info, q, kv_self, kv_anc):
    tile, width = q.shape
    head = kv_self.shape[2] // 2
    keys = (kv_anc.shape[1] + 1) * tile
    return pl.pallas_call(
        forward_kernel,
        out_shape=(
            jax.ShapeDtypeStruct((tile, width), F32),
            jax.ShapeDtypeStruct((tile, width), BF),
            jax.ShapeDtypeStruct((tile, width // head), F32),
        ),
        in_specs=[SMEM_SPEC] + [VMEM_SPEC] * 3,
        out_specs=(VMEM_SPEC,) * 3,
        scratch_shapes=[
            pltpu.VMEM((head, keys), BF),
            pltpu.VMEM((keys, head), BF),
            pltpu.VMEM((1, keys), F32),
        ],
        compiler_params=params(48),
        cost_estimate=cost(8 * tile * keys * width, 2 * (4 * tile * width + 2 * keys * head)),
        name="forward",
    )(info, q, kv_self, kv_anc)


def masked_rows(g_ref, att_ref, at, cols, row_ok):
    g = jnp.where(row_ok, g_ref[at, cols], jnp.zeros((), BF))
    return g, jnp.sum(g.astype(F32) * att_ref[at, cols], axis=1, keepdims=True)


def terms_kernel(
    info_ref, q_ref, g_ref, att_ref, log_ref, anc_ref,
    term_ref,
    kt_ref, vt_ref, bias_ref, dk_ref, dv_ref,
):
    tile, width = q_ref.shape
    head = kt_ref.shape[0]
    heads = width // head
    depth = anc_ref.shape[1]
    length = info_ref[depth]
    load_tiles(None, anc_ref, kt_ref, vt_ref)
    fill_bias(info_ref, bias_ref, tile)
    root = 1.0 / math.sqrt(head)
    for first in range(0, tile, ROWS):
        at = slice(first, first + ROWS)
        row_ok = first + lax.broadcasted_iota(jnp.int32, (ROWS, 1), 0) < length
        for h in range(heads):
            cols = slice(h * head, (h + 1) * head)
            q = q_ref[at, cols]
            g, delta = masked_rows(g_ref, att_ref, at, cols, row_ok)
            s = nn(q, kt_ref[...]) * (LOG2E * root) + bias_ref[...]
            p = jnp.exp2(s - log_ref[at, h : h + 1])
            dp = nn(g, vt_ref[...])
            ds = (p * (dp - delta)).astype(BF)
            dk, dv = tn(ds, q), tn(p.astype(BF), g)
            if first == 0 and h == 0:
                dk_ref[...] = dk
                dv_ref[...] = dv
            else:
                dk_ref[...] += dk
                dv_ref[...] += dv
    for j in range(depth):
        rows = slice(j * tile, (j + 1) * tile)
        shape = (tile // 16, 16, head)
        term_ref[:, j, :, :head] = (dk_ref[rows] * root).astype(BF).reshape(shape)
        term_ref[:, j, :, head:] = dv_ref[rows].astype(BF).reshape(shape)


def ancestor_terms(info, q, g, att, log_total, kv_anc):
    tile, width = q.shape
    head = kv_anc.shape[3] // 2
    keys = kv_anc.shape[1] * tile
    return pl.pallas_call(
        terms_kernel,
        out_shape=jax.ShapeDtypeStruct(kv_anc.shape, BF),
        in_specs=[SMEM_SPEC] + [VMEM_SPEC] * 5,
        out_specs=VMEM_SPEC,
        scratch_shapes=[
            pltpu.VMEM((head, keys), BF),
            pltpu.VMEM((head, keys), BF),
            pltpu.VMEM((1, keys), F32),
            pltpu.VMEM((keys, head), F32),
            pltpu.VMEM((keys, head), F32),
        ],
        compiler_params=params(24),
        cost_estimate=cost(16 * tile * keys * width, 2 * (2 * tile * width + 4 * keys * head)),
        name="ancestor_terms",
    )(info, q, g, att, log_total, kv_anc)


def local_kernel(
    info_ref, q_ref, g_ref, att_ref, log_ref, self_ref, anc_ref,
    dq_ref, own_ref,
    kt_ref, vt_ref, k_ref, bias_ref,
):
    tile, width = q_ref.shape
    head = kt_ref.shape[0]
    heads = width // head
    depth = anc_ref.shape[1]
    length = info_ref[depth]
    load_tiles(self_ref, anc_ref, kt_ref, vt_ref, k_ref)
    fill_bias(info_ref, bias_ref, tile)
    root = 1.0 / math.sqrt(head)
    own_ref[...] = jnp.zeros_like(own_ref)
    for first in range(0, tile, ROWS):
        at = slice(first, first + ROWS)
        own = first + ROWS
        keys = depth * tile + own
        row_ok = first + lax.broadcasted_iota(jnp.int32, (ROWS, 1), 0) < length
        for h in range(heads):
            cols = slice(h * head, (h + 1) * head)
            q = q_ref[at, cols]
            g, delta = masked_rows(g_ref, att_ref, at, cols, row_ok)
            s = block_logits(q, kt_ref, bias_ref, first, keys, tile, LOG2E * root)
            p = jnp.exp2(s - log_ref[at, h : h + 1])
            dp = nn(g, vt_ref[:, :keys])
            ds = (p * (dp - delta)).astype(BF)
            dq_ref[at, cols] = (nn(ds, k_ref[:keys]) * root).astype(BF)
            own_ref[:own, :head] += tn(ds[:, depth * tile :], q)
            own_ref[:own, head:] += tn(p[:, depth * tile :].astype(BF), g)
    own_ref[:, :head] = own_ref[:, :head] * root


def local_grads(info, q, g, att, log_total, kv_self, kv_anc):
    tile, width = q.shape
    head = kv_self.shape[2] // 2
    keys = (kv_anc.shape[1] + 1) * tile
    return pl.pallas_call(
        local_kernel,
        out_shape=(
            jax.ShapeDtypeStruct((tile, width), BF),
            jax.ShapeDtypeStruct((tile, 2 * head), F32),
        ),
        in_specs=[SMEM_SPEC] + [VMEM_SPEC] * 6,
        out_specs=(VMEM_SPEC,) * 2,
        scratch_shapes=[
            pltpu.VMEM((head, keys), BF),
            pltpu.VMEM((head, keys), BF),
            pltpu.VMEM((keys, head), BF),
            pltpu.VMEM((1, keys), F32),
        ],
        compiler_params=params(24),
        cost_estimate=cost(12 * tile * keys * width, 2 * (3 * tile * width + 4 * keys * head)),
        name="local_grads",
    )(info, q, g, att, log_total, kv_self, kv_anc)


def collect_kernel(table_ref, term_ref, rows_ref, out_ref, sum_ref):
    nodes, depth = term_ref.shape[:2]
    width = term_ref.shape[3]
    owner = nodes * depth
    sum_ref[...] = jnp.zeros_like(sum_ref)

    def one_node(n, carry):
        slot = table_ref[owner + n]
        for k in range(depth):
            a = table_ref[n * depth + k]
            target = table_ref[owner + jnp.maximum(a, 0)]
            sum_ref[target] += jnp.where(a >= 0, term_ref[slot, k].astype(F32), 0.0)
        return carry

    lax.fori_loop(0, nodes, one_node, 0, unroll=4)
    out_ref[:, :, :width] = sum_ref[...].astype(BF)
    out_ref[:, :, width:] = rows_ref[...]


def collect(table, terms, rows):
    nodes, chunk, width = terms.shape[0], terms.shape[2], terms.shape[3]
    return pl.pallas_call(
        collect_kernel,
        out_shape=jax.ShapeDtypeStruct((nodes, chunk, width + rows.shape[2]), BF),
        in_specs=[SMEM_SPEC] + [VMEM_SPEC] * 2,
        out_specs=VMEM_SPEC,
        scratch_shapes=[pltpu.VMEM((nodes, chunk, width), F32)],
        compiler_params=params(),
        cost_estimate=cost(0, 4 * terms.size),
        name="collect",
    )(table, terms, rows)


def sum_parts_kernel(*refs):
    parts, out_ref = refs[:-1], refs[-1]
    total = parts[0][...].astype(F32)
    for part in parts[1:]:
        total = total + part[...].astype(F32)
    out_ref[...] = total.astype(BF).T.reshape(out_ref.shape)


def sum_parts(parts, nodes):
    width, rows = parts[0].shape
    return pl.pallas_call(
        sum_parts_kernel,
        out_shape=jax.ShapeDtypeStruct((nodes, rows // nodes, width), BF),
        in_specs=[VMEM_SPEC] * len(parts),
        out_specs=VMEM_SPEC,
        compiler_params=params(),
        cost_estimate=long_cost(),
        name="sum_parts",
    )(*parts)


def finish_kernel(weight_scale, got_ref, own_ref, gk_ref, gv_ref, gw_ref):
    tile, width = own_ref.shape
    head = width // 2
    total = got_ref[:, :, :width].reshape(tile, width).astype(F32) + own_ref[...]
    gk_ref[...] = total[:, :head].astype(BF)
    gv_ref[...] = total[:, head:].astype(BF)
    gw_ref[...] = jnp.sum(got_ref[:, :, width:].astype(F32), axis=0) * weight_scale


def finish(got, own, weight_scale):
    tile, width = own.shape
    return pl.pallas_call(
        lambda *refs: finish_kernel(weight_scale, *refs),
        out_shape=(
            jax.ShapeDtypeStruct((tile, width // 2), BF),
            jax.ShapeDtypeStruct((tile, width // 2), BF),
            jax.ShapeDtypeStruct((got.shape[1], got.shape[2] - width), F32),
        ),
        in_specs=[VMEM_SPEC] * 2,
        out_specs=(VMEM_SPEC,) * 3,
        compiler_params=params(),
        cost_estimate=cost(0, 4 * got.size),
        name="finish",
    )(got, own)


def ring(size, step):
    return [(i, (i + step) % size) for i in range(size)]


def per_device(queries, keys, values, grad_out, out_weight, ancestors, owner, lengths):
    q = queries[0, 0]
    tile, width = q.shape
    head = keys.shape[-1]
    seq = ("z", "y")
    nodes = lax.axis_size(seq)
    xs = lax.axis_size("x")
    core = lax.axis_index("core")
    x = lax.axis_index("x")
    me = lax.axis_index(seq).astype(jnp.int32).reshape(1)

    table = join_tables(ancestors[0], owner[0], lengths[0], me)
    kv_self = join(keys[0, 0], values[0, 0])
    kv_self, out_weight = lax.optimization_barrier((kv_self, out_weight))
    chunks = lax.all_to_all(kv_self, seq, 0, 0, tiled=True)
    def along(rows, step):
        return lax.ppermute(rows, "x", ring(xs, step))

    below, above = along(out_weight, 1), along(out_weight, xs - 1)
    mid = out_weight.shape[0] // 2
    weight = [[out_weight], [below], [along(below[:mid], 1), along(above[mid:], xs - 1)], [above]]
    grads = grad_out[0, 0]
    place = jnp.stack([x, core]).astype(jnp.int32)
    other = other_half(place, grads, xs)
    chunks, other, weight = lax.optimization_barrier((chunks, other, weight))
    sibling = lax.ppermute(other, "core", ring(2, 1))
    routed, info = route(table, chunks, ancestors.shape[2])
    kv_anc = lax.all_to_all(routed, seq, 0, 0, tiled=True)

    blocks = []
    for block in weight:
        blocks += [block, [lax.ppermute(rows, "core", ring(2, 1)) for rows in block]]
    grad_att = grad_attention(place, xs, grads, blocks)

    att, att_low, log_total = forward(info, q, kv_self, kv_anc)
    att_sibling = lax.ppermute(att_low, "core", ring(2, 1))
    terms = ancestor_terms(info, q, grad_att, att, log_total, kv_anc)

    pieces = make_pieces(place, xs, grads, sibling, att_low, att_sibling)
    terms, pieces = lax.optimization_barrier((terms, pieces))
    parts = [pieces[0]] + [lax.ppermute(pieces[k], "x", ring(xs, k)) for k in range(1, xs)]
    terms = lax.all_to_all(terms, seq, 0, 0, tiled=True)
    rows = sum_parts(parts, nodes)
    got = lax.all_to_all(collect(table, terms, rows), seq, 0, 0, tiled=True)
    grad_q, own = local_grads(info, q, grad_att, att, log_total, kv_self, kv_anc)
    token_count = 2 * xs * nodes * tile
    grad_k, grad_v, grad_w = finish(got, own, 1.0 / math.sqrt(token_count))
    return grad_q[None, None], grad_k[None, None], grad_v[None, None], grad_w


def solution(mesh):
    dp, seq = mesh.devices.shape
    fine = Mesh(mesh.devices.reshape(dp // 2, 2, seq // 4, 4), ("x", "core", "z", "y"))
    d, s = ("x", "core"), ("z", "y")
    placed = (
        P(d, s, None, None),
        P(d, s, None, None),
        P(d, s, None, None),
        P(d, s, None, None),
        P(d, None),
        P(d, None, None),
        P(d, None),
        P(d, None),
    )
    return jax.shard_map(
        per_device,
        mesh=fine,
        in_specs=placed,
        out_specs=(
            P(d, s, None, None),
            P(d, s, None, None),
            P(d, s, None, None),
            P(d + s, None),
        ),
        check_vma=False,
    )
```

```python
import math

import jax
import jax.numpy as jnp
from jax import lax
from jax.experimental import pallas as pl
from jax.experimental.pallas import tpu as pltpu
from jax.sharding import Mesh, PartitionSpec as P

BF = jnp.bfloat16
F32 = jnp.float32
MASKED = -1e30
LOG2E = 1.0 / math.log(2.0)
MIB = 1024 * 1024
VMEM_MIB = 8
SMEM_SPEC = pl.BlockSpec(memory_space=pltpu.SMEM)
VMEM_SPEC = pl.BlockSpec(memory_space=pltpu.VMEM)
ROWS = 256


def nn(a, b):
    return lax.dot_general(a, b, (((1,), (0,)), ((), ())), preferred_element_type=F32)


def tn(a, b):
    return lax.dot_general(a, b, (((0,), (0,)), ((), ())), preferred_element_type=F32)


def params(mib=VMEM_MIB):
    return pltpu.CompilerParams(vmem_limit_bytes=mib * MIB)


def cost(flops, moved):
    return pl.CostEstimate(flops=int(flops), bytes_accessed=int(moved), transcendentals=0)


def long_cost():
    return cost(10**13, 10**11)


def join_kernel(k_ref, v_ref, out_ref):
    head = k_ref.shape[2]
    out_ref[:, :, :head] = k_ref[...]
    out_ref[:, :, head:] = v_ref[...]


def join(k, v):
    tile, head = k.shape
    shape = (tile // 16, 16, head)
    return pl.pallas_call(
        join_kernel,
        out_shape=jax.ShapeDtypeStruct((tile // 16, 16, 2 * head), BF),
        in_specs=[VMEM_SPEC] * 2,
        out_specs=VMEM_SPEC,
        compiler_params=params(56),
        cost_estimate=cost(0, 8 * k.size),
        name="join",
    )(k.reshape(shape), v.reshape(shape))


def halves_kernel(place_ref, in_ref, out_ref):
    out_ref[...] = in_ref[...]


def other_half(place, grads, xs):
    tile, features = grads.shape
    block = features // (2 * xs)
    return pl.pallas_call(
        halves_kernel,
        grid_spec=pltpu.PrefetchScalarGridSpec(
            num_scalar_prefetch=1,
            grid=(xs,),
            in_specs=[pl.BlockSpec((tile, block), lambda i, place: (0, 2 * i + 1 - place[1]))],
            out_specs=pl.BlockSpec((tile, block), lambda i, place: (0, i)),
        ),
        out_shape=jax.ShapeDtypeStruct((tile, features // 2), BF),
        compiler_params=params(),
        cost_estimate=long_cost(),
        name="other_half",
    )(place, grads)


def grad_attention_kernel(runs, place_ref, grads_ref, *refs):
    refs, (out_ref, sum_ref) = list(refs[:-2]), refs[-2:]
    step = pl.program_id(0)
    for i, count in enumerate(runs):
        block, refs = refs[:count], refs[count:]

        @pl.when(step == i)
        def _():
            product, first = 0.0, 0
            for rows in block:
                last = first + rows.shape[0]
                product, first = product + nn(grads_ref[:, first:last], rows[...]), last
            if i == 0:
                sum_ref[...] = product
            elif i < len(runs) - 1:
                sum_ref[...] += product
            else:
                out_ref[...] = (sum_ref[...] + product).astype(BF)


def grad_attention(place, xs, grads, blocks):
    tile, features = grads.shape
    runs = [rows for block in blocks for rows in block]
    width = runs[0].shape[1]
    block = features // (2 * xs)

    def column(i, place):
        source = lax.rem(place[0] + xs - lax.div(i, 2), xs)
        return 0, 2 * source + lax.rem(place[1] + i, 2)

    return pl.pallas_call(
        lambda *refs: grad_attention_kernel([len(block) for block in blocks], *refs),
        grid_spec=pltpu.PrefetchScalarGridSpec(
            num_scalar_prefetch=1,
            grid=(2 * xs,),
            in_specs=[pl.BlockSpec((tile, block), column)]
            + [pl.BlockSpec(rows.shape, lambda i, place: (0, 0)) for rows in runs],
            out_specs=pl.BlockSpec((tile, width), lambda i, place: (0, 0)),
            scratch_shapes=[pltpu.VMEM((tile, width), F32)],
        ),
        out_shape=jax.ShapeDtypeStruct((tile, width), BF),
        compiler_params=params(16),
        cost_estimate=cost(2 * tile * features * width, 2 * (tile + width) * features),
        name="grad_attention",
    )(place, grads, *runs)


def pieces_kernel(
    place_ref, grads_ref, sibling_ref, att_ref, att_sibling_ref,
    own_ref, up_ref, opposite_low_ref, opposite_high_ref, down_ref,
):
    width, block = own_ref.shape
    xs = sibling_ref.shape[1] // block
    mine_t, sibling_t = att_ref[...].T, att_sibling_ref[...].T
    outs = ([own_ref], [up_ref], [opposite_low_ref, opposite_high_ref], [down_ref])
    for k in (2, 1, 3, 0):
        at = lax.rem(place_ref[0] + k, xs)
        mine = grads_ref[:, pl.ds(pl.multiple_of((2 * at + place_ref[1]) * block, block), block)]
        sibling = sibling_ref[:, pl.ds(pl.multiple_of(at * block, block), block)]
        total = (nn(mine_t, mine) + nn(sibling_t, sibling)).astype(BF)
        first = 0
        for out_ref in outs[k]:
            out_ref[...] = total[first : first + out_ref.shape[0]]
            first += out_ref.shape[0]


def make_pieces(place, xs, grads, sibling, att, att_sibling):
    tile, features = grads.shape
    block = features // (2 * xs)
    width = att.shape[1]
    whole = jax.ShapeDtypeStruct((width, block), BF)
    half = jax.ShapeDtypeStruct((width // 2, block), BF)
    return pl.pallas_call(
        pieces_kernel,
        out_shape=(whole, whole, half, half, whole),
        in_specs=[SMEM_SPEC] + [VMEM_SPEC] * 4,
        out_specs=(VMEM_SPEC,) * 5,
        compiler_params=params(24),
        cost_estimate=cost(4 * tile * block * width * xs, 2 * xs * (2 * tile * block + block * width)),
        name="pieces",
    )(place, grads, sibling, att, att_sibling)


def fold_kernel(up_ref, from_below_ref, down_ref, from_above_ref, up_out_ref, down_out_ref):
    half = from_below_ref.shape[0]

    def add(a, b):
        return (a.astype(F32) + b.astype(F32)).astype(BF)

    up_out_ref[:half] = add(up_ref[:half], from_below_ref[...])
    up_out_ref[half:] = up_ref[half:]
    down_out_ref[:half] = down_ref[:half]
    down_out_ref[half:] = add(down_ref[half:], from_above_ref[...])


def fold(up, from_below, down, from_above):
    shape = jax.ShapeDtypeStruct(up.shape, BF)
    return pl.pallas_call(
        fold_kernel,
        out_shape=(shape, shape),
        in_specs=[VMEM_SPEC] * 4,
        out_specs=(VMEM_SPEC, VMEM_SPEC),
        compiler_params=params(),
        cost_estimate=long_cost(),
        name="fold",
    )(up, from_below, down, from_above)


def join_tables(anc, owner, lengths, me):
    return jnp.concatenate([anc.reshape(-1), owner, lengths, me])


def route_kernel(table_ref, chunk_ref, out_ref, info_ref):
    nodes, depth = out_ref.shape[:2]
    owner, lengths = nodes * depth, nodes * (depth + 1)
    me = table_ref[nodes * (depth + 2)]
    zero = jnp.zeros(out_ref.shape[2:], out_ref.dtype)

    def one_node(n, mine):
        slot = table_ref[owner + n]
        for k in range(depth):
            a = table_ref[n * depth + k]
            source = table_ref[owner + jnp.maximum(a, 0)]
            out_ref[slot, k] = jnp.where(a >= 0, chunk_ref[source], zero)
        return jnp.where(slot == me, n, mine)

    mine = lax.fori_loop(0, nodes, one_node, 0, unroll=4)
    for k in range(depth):
        a = table_ref[mine * depth + k]
        info_ref[k] = jnp.where(a >= 0, table_ref[lengths + jnp.maximum(a, 0)], 0)
    info_ref[depth] = table_ref[lengths + mine]


def route(table, chunks, depth):
    nodes = chunks.shape[0]
    return pl.pallas_call(
        route_kernel,
        out_shape=(
            jax.ShapeDtypeStruct((nodes, depth) + chunks.shape[1:], BF),
            jax.ShapeDtypeStruct((depth + 1,), jnp.int32),
        ),
        in_specs=[SMEM_SPEC, VMEM_SPEC],
        out_specs=(VMEM_SPEC, SMEM_SPEC),
        compiler_params=params(),
        cost_estimate=long_cost(),
        name="route",
    )(table, chunks)


def load_tiles(self_ref, anc_ref, kt_ref, vt_ref, k_ref):
    head = kt_ref.shape[0]
    depth = anc_ref.shape[1]
    tile = anc_ref.shape[0] * anc_ref.shape[2]
    for j in range(depth + 1):
        kv = (anc_ref[:, j] if j < depth else self_ref[...]).reshape(tile, 2 * head)
        k_part, v_part = kv[:, :head], kv[:, head:]
        at = slice(j * tile, (j + 1) * tile)
        kt_ref[:, at] = k_part.T
        vt_ref[:, at] = v_part.T
        k_ref[at] = k_part


def fill_bias(info_ref, bias_ref, tile):
    tiles = bias_ref.shape[1] // tile
    pos = lax.broadcasted_iota(jnp.int32, (1, tile), 1)
    for j in range(tiles):
        bias_ref[:, j * tile : (j + 1) * tile] = jnp.where(pos < info_ref[j], 0.0, MASKED)


def block_logits(q, kt_ref, bias_ref, first, width, tile, scale):
    s = nn(q, kt_ref[:, :width]) * scale + bias_ref[:, :width]
    base = kt_ref.shape[1] - tile + first
    q_pos = lax.broadcasted_iota(jnp.int32, (ROWS, ROWS), 0)
    k_pos = lax.broadcasted_iota(jnp.int32, (ROWS, ROWS), 1)
    diagonal = jnp.where(k_pos <= q_pos, s[:, base : base + ROWS], MASKED)
    return jnp.concatenate([s[:, :base], diagonal], axis=1)


def forward_kernel(
    info_ref, q_ref, self_ref, anc_ref, att_ref, low_ref, log_ref, k_ref, vt_ref, qt_ref, bias_ref
):
    tile, width = q_ref.shape
    head = vt_ref.shape[0]
    depth = anc_ref.shape[1]
    scale = LOG2E / math.sqrt(head)
    qt_ref[...] = q_ref[...].T
    pos = lax.broadcasted_iota(jnp.int32, (tile, tile), 0)
    for j in range(depth + 1):
        kv = (anc_ref[:, j] if j < depth else self_ref[...]).reshape(tile, 2 * head)
        rows = slice(j * tile, (j + 1) * tile)
        k_ref[rows] = kv[:, :head]
        vt_ref[:, rows] = kv[:, head:].T
        visible = pos < info_ref[j]
        if j == depth:
            visible = visible & (pos <= lax.broadcasted_iota(jnp.int32, (tile, tile), 1))
        bias_ref[rows] = jnp.where(visible, 0.0, MASKED)
    row_ok = lax.broadcasted_iota(jnp.int32, (tile, 1), 0) < info_ref[depth]
    for h in range(width // head):
        cols = slice(h * head, (h + 1) * head)
        s = nn(k_ref[...], qt_ref[cols]) * scale + bias_ref[...]
        top = jnp.max(s, axis=0, keepdims=True)
        w = jnp.exp2(s - top)
        total = jnp.sum(w, axis=0, keepdims=True)
        att = (nn(vt_ref[...], w.astype(BF)) / total).T
        att_ref[:, cols] = att
        low_ref[:, cols] = jnp.where(row_ok, att, 0.0).astype(BF)
        log_ref[h : h + 1] = top + jnp.log2(total)


def forward(info, q, kv_self, kv_anc):
    tile, width = q.shape
    head = kv_self.shape[2] // 2
    keys = (kv_anc.shape[1] + 1) * tile
    return pl.pallas_call(
        forward_kernel,
        out_shape=(
            jax.ShapeDtypeStruct((tile, width), F32),
            jax.ShapeDtypeStruct((tile, width), BF),
            jax.ShapeDtypeStruct((width // head, tile), F32),
        ),
        in_specs=[SMEM_SPEC] + [VMEM_SPEC] * 3,
        out_specs=(VMEM_SPEC,) * 3,
        scratch_shapes=[
            pltpu.VMEM((keys, head), BF),
            pltpu.VMEM((head, keys), BF),
            pltpu.VMEM((width, tile), BF),
            pltpu.VMEM((keys, tile), F32),
        ],
        compiler_params=params(40),
        cost_estimate=cost(8 * tile * keys * width, 2 * (4 * tile * width + 2 * keys * head)),
        name="forward",
    )(info, q, kv_self, kv_anc)


def masked_rows(g_ref, att_ref, at, cols, row_ok):
    g = jnp.where(row_ok, g_ref[at, cols], jnp.zeros((), BF))
    return g, jnp.sum(g.astype(F32) * att_ref[at, cols], axis=1, keepdims=True)


def terms_kernel(
    info_ref, q_ref, g_ref, att_ref, log_ref, anc_ref,
    term_ref,
    k_ref, v_ref, qt_ref, gm_ref, gt_ref, stat_ref, dk_ref, dv_ref,
):
    tile, width = q_ref.shape
    head = k_ref.shape[1]
    heads = width // head
    depth = anc_ref.shape[1]
    root = 1.0 / math.sqrt(head)
    pos = lax.broadcasted_iota(jnp.int32, (tile, 1), 0)
    masked = jnp.where(pos < info_ref[depth], g_ref[...], jnp.zeros((), BF))
    gm_ref[...] = masked
    gt_ref[...] = masked.T
    qt_ref[...] = q_ref[...].T
    for h in range(heads):
        cols = slice(h * head, (h + 1) * head)
        delta = jnp.sum(masked[:, cols].astype(F32) * att_ref[:, cols], axis=1, keepdims=True)
        stat_ref[h : h + 1] = delta.T
    for j in range(depth):
        kv = anc_ref[:, j].reshape(tile, 2 * head)
        rows = slice(j * tile, (j + 1) * tile)
        k_ref[rows] = kv[:, :head]
        v_ref[rows] = kv[:, head:]
    for first in range(0, tile, ROWS):
        at = slice(first, first + ROWS)
        for h in range(heads):
            cols = slice(h * head, (h + 1) * head)
            p = jnp.exp2(nn(k_ref[...], qt_ref[cols, at]) * (LOG2E * root) - log_ref[h : h + 1, at])
            dp = nn(v_ref[...], gt_ref[cols, at])
            ds = (p * (dp - stat_ref[h : h + 1, at])).astype(BF)
            dk, dv = nn(ds, q_ref[at, cols]), nn(p.astype(BF), gm_ref[at, cols])
            if first == 0 and h == 0:
                dk_ref[...] = dk
                dv_ref[...] = dv
            else:
                dk_ref[...] += dk
                dv_ref[...] += dv
    for j in range(depth):
        rows = slice(j * tile, (j + 1) * tile)
        shape = (tile // 16, 16, head)
        visible = pos < info_ref[j]
        term_ref[:, j, :, :head] = jnp.where(visible, dk_ref[rows] * root, 0.0).astype(BF).reshape(shape)
        term_ref[:, j, :, head:] = jnp.where(visible, dv_ref[rows], 0.0).astype(BF).reshape(shape)


def ancestor_terms(info, q, g, att, log_total, kv_anc):
    tile, width = q.shape
    head = kv_anc.shape[3] // 2
    keys = kv_anc.shape[1] * tile
    return pl.pallas_call(
        terms_kernel,
        out_shape=jax.ShapeDtypeStruct(kv_anc.shape, BF),
        in_specs=[SMEM_SPEC] + [VMEM_SPEC] * 5,
        out_specs=VMEM_SPEC,
        scratch_shapes=[
            pltpu.VMEM((keys, head), BF),
            pltpu.VMEM((keys, head), BF),
            pltpu.VMEM((width, tile), BF),
            pltpu.VMEM((tile, width), BF),
            pltpu.VMEM((width, tile), BF),
            pltpu.VMEM((width // head, tile), F32),
            pltpu.VMEM((keys, head), F32),
            pltpu.VMEM((keys, head), F32),
        ],
        compiler_params=params(24),
        cost_estimate=cost(16 * tile * keys * width, 2 * (2 * tile * width + 4 * keys * head)),
        name="ancestor_terms",
    )(info, q, g, att, log_total, kv_anc)


def local_kernel(
    info_ref, q_ref, g_ref, att_ref, log_ref, self_ref, anc_ref,
    dq_ref, own_ref,
    kt_ref, vt_ref, k_ref, bias_ref,
):
    tile, width = q_ref.shape
    head = kt_ref.shape[0]
    heads = width // head
    depth = anc_ref.shape[1]
    length = info_ref[depth]
    load_tiles(self_ref, anc_ref, kt_ref, vt_ref, k_ref)
    fill_bias(info_ref, bias_ref, tile)
    root = 1.0 / math.sqrt(head)
    own_ref[...] = jnp.zeros_like(own_ref)
    log_total = log_ref[...].T
    for first in range(0, tile, ROWS):
        at = slice(first, first + ROWS)
        own = first + ROWS
        keys = depth * tile + own
        row_ok = first + lax.broadcasted_iota(jnp.int32, (ROWS, 1), 0) < length
        for h in range(heads):
            cols = slice(h * head, (h + 1) * head)
            q = q_ref[at, cols]
            g, delta = masked_rows(g_ref, att_ref, at, cols, row_ok)
            s = block_logits(q, kt_ref, bias_ref, first, keys, tile, LOG2E * root)
            p = jnp.exp2(s - log_total[at, h : h + 1])
            dp = nn(g, vt_ref[:, :keys])
            ds = (p * (dp - delta)).astype(BF)
            dq_ref[at, cols] = (nn(ds, k_ref[:keys]) * root).astype(BF)
            own_ref[:own, :head] += tn(ds[:, depth * tile :], q)
            own_ref[:own, head:] += tn(p[:, depth * tile :].astype(BF), g)
    own_ref[:, :head] = own_ref[:, :head] * root


def local_grads(info, q, g, att, log_total, kv_self, kv_anc):
    tile, width = q.shape
    head = kv_self.shape[2] // 2
    keys = (kv_anc.shape[1] + 1) * tile
    return pl.pallas_call(
        local_kernel,
        out_shape=(
            jax.ShapeDtypeStruct((tile, width), BF),
            jax.ShapeDtypeStruct((tile, 2 * head), F32),
        ),
        in_specs=[SMEM_SPEC] + [VMEM_SPEC] * 6,
        out_specs=(VMEM_SPEC,) * 2,
        scratch_shapes=[
            pltpu.VMEM((head, keys), BF),
            pltpu.VMEM((head, keys), BF),
            pltpu.VMEM((keys, head), BF),
            pltpu.VMEM((1, keys), F32),
        ],
        compiler_params=params(24),
        cost_estimate=cost(12 * tile * keys * width, 2 * (3 * tile * width + 4 * keys * head)),
        name="local_grads",
    )(info, q, g, att, log_total, kv_self, kv_anc)


def collect_kernel(table_ref, term_ref, keep_ref, came_ref, out_ref, sum_ref):
    nodes, depth = term_ref.shape[:2]
    width = term_ref.shape[3]
    owner = nodes * depth
    sum_ref[...] = jnp.zeros_like(sum_ref)

    def one_node(n, carry):
        slot = table_ref[owner + n]
        for k in range(depth):
            a = table_ref[n * depth + k]
            target = table_ref[owner + jnp.maximum(a, 0)]
            sum_ref[target] += jnp.where(a >= 0, term_ref[slot, k].astype(F32), 0.0)
        return carry

    lax.fori_loop(0, nodes, one_node, 0, unroll=4)
    out_ref[:, :, :width] = sum_ref[...].astype(BF)
    out_ref[:, :, width:] = (keep_ref[...] + came_ref[...].astype(F32)).astype(BF)


def collect(table, terms, keep, came):
    nodes, chunk, width = terms.shape[0], terms.shape[2], terms.shape[3]
    return pl.pallas_call(
        collect_kernel,
        out_shape=jax.ShapeDtypeStruct((nodes, chunk, width + keep.shape[2]), BF),
        in_specs=[SMEM_SPEC] + [VMEM_SPEC] * 3,
        out_specs=VMEM_SPEC,
        scratch_shapes=[pltpu.VMEM((nodes, chunk, width), F32)],
        compiler_params=params(),
        cost_estimate=cost(0, 4 * terms.size),
        name="collect",
    )(table, terms, keep, came)


def sum_parts_kernel(odd_ref, *refs):
    parts, (keep_ref, send_ref) = refs[:-2], refs[-2:]
    half = keep_ref.shape[2]
    for out_ref, first in ((keep_ref, odd_ref[0] * half), (send_ref, (1 - odd_ref[0]) * half)):
        at = pl.ds(pl.multiple_of(first, half), half)
        total = parts[0][at, :].astype(F32)
        for part in parts[1:]:
            total = total + part[at, :].astype(F32)
        out_ref[...] = total.astype(out_ref.dtype).T.reshape(out_ref.shape)


def sum_parts(odd, parts, nodes):
    width, rows = parts[0].shape
    shape = (nodes, rows // nodes, width // 2)
    return pl.pallas_call(
        sum_parts_kernel,
        out_shape=(jax.ShapeDtypeStruct(shape, F32), jax.ShapeDtypeStruct(shape, BF)),
        in_specs=[SMEM_SPEC] + [VMEM_SPEC] * len(parts),
        out_specs=(VMEM_SPEC, VMEM_SPEC),
        compiler_params=params(12),
        cost_estimate=cost(0, 10 * rows * width),
        name="sum_parts",
    )(odd, *parts)


def finish_kernel(weight_scale, got_ref, own_ref, gk_ref, gv_ref, gw_ref):
    tile, width = own_ref.shape
    head = width // 2
    total = got_ref[:, :, :width].reshape(tile, width).astype(F32) + own_ref[...]
    gk_ref[...] = total[:, :head].astype(BF)
    gv_ref[...] = total[:, head:].astype(BF)
    nodes, rows, half = got_ref.shape[0], got_ref.shape[1], got_ref.shape[2] - width
    sent = got_ref[:, :, width:].astype(F32).reshape(nodes // 2, 2, rows, half)
    sums = jnp.sum(sent, axis=0) * weight_scale
    gw_ref[:, :half] = sums[0]
    gw_ref[:, half:] = sums[1]


def finish(got, own, weight_scale):
    tile, width = own.shape
    return pl.pallas_call(
        lambda *refs: finish_kernel(weight_scale, *refs),
        out_shape=(
            jax.ShapeDtypeStruct((tile, width // 2), BF),
            jax.ShapeDtypeStruct((tile, width // 2), BF),
            jax.ShapeDtypeStruct((got.shape[1], 2 * (got.shape[2] - width)), F32),
        ),
        in_specs=[VMEM_SPEC] * 2,
        out_specs=(VMEM_SPEC,) * 3,
        compiler_params=params(),
        cost_estimate=cost(0, 4 * got.size),
        name="finish",
    )(got, own)


def ring(size, step):
    return [(i, (i + step) % size) for i in range(size)]


def per_device(queries, keys, values, grad_out, out_weight, ancestors, owner, lengths):
    q = queries[0, 0]
    tile, width = q.shape
    head = keys.shape[-1]
    seq = ("z", "y")
    nodes = lax.axis_size(seq)
    xs = lax.axis_size("x")
    core = lax.axis_index("core")
    x = lax.axis_index("x")
    me = lax.axis_index(seq).astype(jnp.int32).reshape(1)

    table = join_tables(ancestors[0], owner[0], lengths[0], me)
    kv_self = join(keys[0, 0], values[0, 0])
    kv_self, out_weight = lax.optimization_barrier((kv_self, out_weight))
    chunks = lax.all_to_all(kv_self, seq, 0, 0, tiled=True)
    def along(rows, step):
        return lax.ppermute(rows, "x", ring(xs, step))

    below, above = along(out_weight, 1), along(out_weight, xs - 1)
    mid = out_weight.shape[0] // 2
    weight = [[out_weight], [below], [along(below[:mid], 1), along(above[mid:], xs - 1)], [above]]
    grads = grad_out[0, 0]
    place = jnp.stack([x, core]).astype(jnp.int32)
    other = other_half(place, grads, xs)
    chunks, other, weight[:2], weight[3:] = lax.optimization_barrier(
        (chunks, other, weight[:2], weight[3:])
    )
    sibling = lax.ppermute(other, "core", ring(2, 1))
    routed, info = route(table, chunks, ancestors.shape[2])
    kv_anc = lax.all_to_all(routed, seq, 0, 0, tiled=True)

    blocks = []
    for block in weight:
        blocks += [block, [lax.ppermute(rows, "core", ring(2, 1)) for rows in block]]
    grad_att = grad_attention(place, xs, grads, blocks)

    att, att_low, log_total = forward(info, q, kv_self, kv_anc)
    att_sibling = lax.ppermute(att_low, "core", ring(2, 1))
    terms = ancestor_terms(info, q, grad_att, att, log_total, kv_anc)

    pieces = make_pieces(place, xs, grads, sibling, att_low, att_sibling)
    terms, pieces = lax.optimization_barrier((terms, pieces))
    own_piece, up, opposite_low, opposite_high, down = pieces
    from_below, from_above = along(opposite_low, 1), along(opposite_high, xs - 1)
    up, down = fold(up, from_below, down, from_above)
    parts = [own_piece, along(up, 1), along(down, xs - 1)]
    terms = lax.all_to_all(terms, seq, 0, 0, tiled=True)
    odd = lax.rem(lax.axis_index("y"), 2).astype(jnp.int32).reshape(1)
    keep, send = sum_parts(odd, parts, nodes)
    came = lax.ppermute(send, "y", [(i, i ^ 1) for i in range(lax.axis_size("y"))])
    got = lax.all_to_all(collect(table, terms, keep, came), seq, 0, 0, tiled=True)
    grad_q, own = local_grads(info, q, grad_att, att, log_total, kv_self, kv_anc)
    token_count = 2 * xs * nodes * tile
    grad_k, grad_v, grad_w = finish(got, own, 1.0 / math.sqrt(token_count))
    return grad_q[None, None], grad_k[None, None], grad_v[None, None], grad_w


def solution(mesh):
    dp, seq = mesh.devices.shape
    fine = Mesh(mesh.devices.reshape(dp // 2, 2, seq // 4, 4), ("x", "core", "z", "y"))
    d, s = ("x", "core"), ("z", "y")
    placed = (
        P(d, s, None, None),
        P(d, s, None, None),
        P(d, s, None, None),
        P(d, s, None, None),
        P(d, None),
        P(d, None, None),
        P(d, None),
        P(d, None),
    )
    return jax.shard_map(
        per_device,
        mesh=fine,
        in_specs=placed,
        out_specs=(
            P(d, s, None, None),
            P(d, s, None, None),
            P(d, s, None, None),
            P(d + s, None),
        ),
        check_vma=False,
    )
```

```python
import math

import jax
import jax.numpy as jnp
from jax import lax
from jax.experimental import pallas as pl
from jax.experimental.pallas import tpu as pltpu
from jax.sharding import Mesh, PartitionSpec as P

BF = jnp.bfloat16
F32 = jnp.float32
MASKED = -1e30
LOG2E = 1.0 / math.log(2.0)
MIB = 1024 * 1024
VMEM_MIB = 8
SMEM_SPEC = pl.BlockSpec(memory_space=pltpu.SMEM)
VMEM_SPEC = pl.BlockSpec(memory_space=pltpu.VMEM)
HBM_SPEC = pl.BlockSpec(memory_space=pltpu.HBM)
ROWS = 256


def nn(a, b):
    return lax.dot_general(a, b, (((1,), (0,)), ((), ())), preferred_element_type=F32)


def tn(a, b):
    return lax.dot_general(a, b, (((0,), (0,)), ((), ())), preferred_element_type=F32)


def params(mib=VMEM_MIB):
    return pltpu.CompilerParams(vmem_limit_bytes=mib * MIB)


def cost(flops, moved):
    return pl.CostEstimate(flops=int(flops), bytes_accessed=int(moved), transcendentals=0)


def long_cost():
    return cost(10**13, 10**11)


def join_kernel(k_ref, v_ref, out_ref):
    head = k_ref.shape[2]
    out_ref[:, :, :head] = k_ref[...]
    out_ref[:, :, head:] = v_ref[...]


def join(k, v):
    tile, head = k.shape
    shape = (tile // 16, 16, head)
    return pl.pallas_call(
        join_kernel,
        out_shape=jax.ShapeDtypeStruct((tile // 16, 16, 2 * head), BF),
        in_specs=[VMEM_SPEC] * 2,
        out_specs=VMEM_SPEC,
        compiler_params=params(56),
        cost_estimate=cost(0, 8 * k.size),
        name="join",
    )(k.reshape(shape), v.reshape(shape))


def halves_kernel(place_ref, in_ref, out_ref):
    out_ref[...] = in_ref[...]


def other_half(place, grads, xs):
    tile, features = grads.shape
    block = features // (2 * xs)
    return pl.pallas_call(
        halves_kernel,
        grid_spec=pltpu.PrefetchScalarGridSpec(
            num_scalar_prefetch=1,
            grid=(xs,),
            in_specs=[pl.BlockSpec((tile, block), lambda i, place: (0, 2 * i + 1 - place[1]))],
            out_specs=pl.BlockSpec((tile, block), lambda i, place: (0, i)),
        ),
        out_shape=jax.ShapeDtypeStruct((tile, features // 2), BF),
        compiler_params=params(),
        cost_estimate=long_cost(),
        name="other_half",
    )(place, grads)


def grad_attention_kernel(runs, place_ref, grads_ref, *refs):
    count = sum(runs)
    refs, (out_ref, grads_stage, weight_stage, sems) = refs[:count], refs[count:]
    rows_each = weight_stage.shape[1]
    xs = len(runs) // 2
    blocks, refs = [], list(refs)
    for i, run in enumerate(runs):
        source = 2 * lax.rem(place_ref[0] + xs - i // 2, xs) + lax.rem(place_ref[1] + i % 2, 2)
        at = pl.ds(pl.multiple_of(source * rows_each, rows_each), rows_each)
        loads = [pltpu.make_async_copy(grads_ref.at[:, at], grads_stage.at[i], sems.at[i, 0])]
        first = 0
        for part, rows in enumerate(refs[:run]):
            to = weight_stage.at[i, pl.ds(first, rows.shape[0])]
            loads.append(pltpu.make_async_copy(rows, to, sems.at[i, 1 + part]))
            first += rows.shape[0]
        refs = refs[run:]
        for load in loads:
            load.start()
        blocks.append(loads)
    total = 0.0
    for i, loads in enumerate(blocks):
        for load in loads:
            load.wait()
        total = total + nn(grads_stage[i], weight_stage[i])
    out_ref[...] = total.astype(BF)


def grad_attention(place, grads, blocks):
    tile, features = grads.shape
    runs = [rows for block in blocks for rows in block]
    width = runs[0].shape[1]
    each = features // len(blocks)
    return pl.pallas_call(
        lambda *refs: grad_attention_kernel([len(block) for block in blocks], *refs),
        out_shape=jax.ShapeDtypeStruct((tile, width), BF),
        in_specs=[SMEM_SPEC] + [HBM_SPEC] * (1 + len(runs)),
        out_specs=VMEM_SPEC,
        scratch_shapes=[
            pltpu.VMEM((len(blocks), tile, each), BF),
            pltpu.VMEM((len(blocks), each, width), BF),
            pltpu.SemaphoreType.DMA((len(blocks), 3)),
        ],
        compiler_params=params(56),
        cost_estimate=cost(2 * tile * features * width, 2 * (tile + width) * features),
        name="grad_attention",
    )(place, grads, *runs)


def pieces_kernel(
    place_ref, grads_ref, sibling_ref, att_ref, att_sibling_ref,
    own_ref, up_ref, opposite_low_ref, opposite_high_ref, down_ref,
):
    width, block = own_ref.shape
    xs = sibling_ref.shape[1] // block
    mine_t, sibling_t = att_ref[...].T, att_sibling_ref[...].T
    outs = ([own_ref], [up_ref], [opposite_low_ref, opposite_high_ref], [down_ref])
    for k in (2, 1, 3, 0):
        at = lax.rem(place_ref[0] + k, xs)
        mine = grads_ref[:, pl.ds(pl.multiple_of((2 * at + place_ref[1]) * block, block), block)]
        sibling = sibling_ref[:, pl.ds(pl.multiple_of(at * block, block), block)]
        total = (nn(mine_t, mine) + nn(sibling_t, sibling)).astype(BF)
        first = 0
        for out_ref in outs[k]:
            out_ref[...] = total[first : first + out_ref.shape[0]]
            first += out_ref.shape[0]


def make_pieces(place, xs, grads, sibling, att, att_sibling):
    tile, features = grads.shape
    block = features // (2 * xs)
    width = att.shape[1]
    whole = jax.ShapeDtypeStruct((width, block), BF)
    half = jax.ShapeDtypeStruct((width // 2, block), BF)
    return pl.pallas_call(
        pieces_kernel,
        out_shape=(whole, whole, half, half, whole),
        in_specs=[SMEM_SPEC] + [VMEM_SPEC] * 4,
        out_specs=(VMEM_SPEC,) * 5,
        compiler_params=params(24),
        cost_estimate=cost(4 * tile * block * width * xs, 2 * xs * (2 * tile * block + block * width)),
        name="pieces",
    )(place, grads, sibling, att, att_sibling)


def fold_kernel(up_ref, from_below_ref, down_ref, from_above_ref, up_out_ref, down_out_ref):
    half = from_below_ref.shape[0]

    def add(a, b):
        return (a.astype(F32) + b.astype(F32)).astype(BF)

    up_out_ref[:half] = add(up_ref[:half], from_below_ref[...])
    up_out_ref[half:] = up_ref[half:]
    down_out_ref[:half] = down_ref[:half]
    down_out_ref[half:] = add(down_ref[half:], from_above_ref[...])


def fold(up, from_below, down, from_above):
    shape = jax.ShapeDtypeStruct(up.shape, BF)
    return pl.pallas_call(
        fold_kernel,
        out_shape=(shape, shape),
        in_specs=[VMEM_SPEC] * 4,
        out_specs=(VMEM_SPEC, VMEM_SPEC),
        compiler_params=params(),
        cost_estimate=long_cost(),
        name="fold",
    )(up, from_below, down, from_above)


def join_tables(anc, owner, lengths, me):
    return jnp.concatenate([anc.reshape(-1), owner, lengths, me])


def route_kernel(table_ref, chunk_ref, out_ref, info_ref):
    nodes, depth = out_ref.shape[:2]
    owner, lengths = nodes * depth, nodes * (depth + 1)
    me = table_ref[nodes * (depth + 2)]
    zero = jnp.zeros(out_ref.shape[2:], out_ref.dtype)

    def one_node(n, mine):
        slot = table_ref[owner + n]
        for k in range(depth):
            a = table_ref[n * depth + k]
            source = table_ref[owner + jnp.maximum(a, 0)]
            out_ref[slot, k] = jnp.where(a >= 0, chunk_ref[source], zero)
        return jnp.where(slot == me, n, mine)

    mine = lax.fori_loop(0, nodes, one_node, 0, unroll=4)
    for k in range(depth):
        a = table_ref[mine * depth + k]
        info_ref[k] = jnp.where(a >= 0, table_ref[lengths + jnp.maximum(a, 0)], 0)
    info_ref[depth] = table_ref[lengths + mine]


def route(table, chunks, depth):
    nodes = chunks.shape[0]
    return pl.pallas_call(
        route_kernel,
        out_shape=(
            jax.ShapeDtypeStruct((nodes, depth) + chunks.shape[1:], BF),
            jax.ShapeDtypeStruct((depth + 1,), jnp.int32),
        ),
        in_specs=[SMEM_SPEC, VMEM_SPEC],
        out_specs=(VMEM_SPEC, SMEM_SPEC),
        compiler_params=params(),
        cost_estimate=long_cost(),
        name="route",
    )(table, chunks)


def load_tiles(self_ref, anc_ref, kt_ref, vt_ref, k_ref):
    head = kt_ref.shape[0]
    depth = anc_ref.shape[1]
    tile = anc_ref.shape[0] * anc_ref.shape[2]
    for j in range(depth + 1):
        kv = (anc_ref[:, j] if j < depth else self_ref[...]).reshape(tile, 2 * head)
        k_part, v_part = kv[:, :head], kv[:, head:]
        at = slice(j * tile, (j + 1) * tile)
        kt_ref[:, at] = k_part.T
        vt_ref[:, at] = v_part.T
        k_ref[at] = k_part


def fill_bias(info_ref, bias_ref, tile):
    tiles = bias_ref.shape[1] // tile
    pos = lax.broadcasted_iota(jnp.int32, (1, tile), 1)
    for j in range(tiles):
        bias_ref[:, j * tile : (j + 1) * tile] = jnp.where(pos < info_ref[j], 0.0, MASKED)


def block_logits(q, kt_ref, bias_ref, first, width, tile, scale):
    s = nn(q, kt_ref[:, :width]) * scale + bias_ref[:, :width]
    base = kt_ref.shape[1] - tile + first
    q_pos = lax.broadcasted_iota(jnp.int32, (ROWS, ROWS), 0)
    k_pos = lax.broadcasted_iota(jnp.int32, (ROWS, ROWS), 1)
    diagonal = jnp.where(k_pos <= q_pos, s[:, base : base + ROWS], MASKED)
    return jnp.concatenate([s[:, :base], diagonal], axis=1)


def forward_kernel(
    info_ref, q_ref, self_ref, anc_ref, att_ref, low_ref, log_ref, k_ref, vt_ref, qt_ref, bias_ref
):
    tile, width = q_ref.shape
    head = vt_ref.shape[0]
    depth = anc_ref.shape[1]
    scale = LOG2E / math.sqrt(head)
    qt_ref[...] = q_ref[...].T
    pos = lax.broadcasted_iota(jnp.int32, (tile, tile), 0)
    for j in range(depth + 1):
        kv = (anc_ref[:, j] if j < depth else self_ref[...]).reshape(tile, 2 * head)
        rows = slice(j * tile, (j + 1) * tile)
        k_ref[rows] = kv[:, :head]
        vt_ref[:, rows] = kv[:, head:].T
        visible = pos < info_ref[j]
        if j == depth:
            visible = visible & (pos <= lax.broadcasted_iota(jnp.int32, (tile, tile), 1))
        bias_ref[rows] = jnp.where(visible, 0.0, MASKED)
    row_ok = lax.broadcasted_iota(jnp.int32, (tile, 1), 0) < info_ref[depth]
    for h in range(width // head):
        cols = slice(h * head, (h + 1) * head)
        s = nn(k_ref[...], qt_ref[cols]) * scale + bias_ref[...]
        top = jnp.max(s, axis=0, keepdims=True)
        w = jnp.exp2(s - top)
        total = jnp.sum(w, axis=0, keepdims=True)
        att = (nn(vt_ref[...], w.astype(BF)) / total).T
        att_ref[:, cols] = att
        low_ref[:, cols] = jnp.where(row_ok, att, 0.0).astype(BF)
        log_ref[h : h + 1] = top + jnp.log2(total)


def forward(info, q, kv_self, kv_anc):
    tile, width = q.shape
    head = kv_self.shape[2] // 2
    keys = (kv_anc.shape[1] + 1) * tile
    return pl.pallas_call(
        forward_kernel,
        out_shape=(
            jax.ShapeDtypeStruct((tile, width), F32),
            jax.ShapeDtypeStruct((tile, width), BF),
            jax.ShapeDtypeStruct((width // head, tile), F32),
        ),
        in_specs=[SMEM_SPEC] + [VMEM_SPEC] * 3,
        out_specs=(VMEM_SPEC,) * 3,
        scratch_shapes=[
            pltpu.VMEM((keys, head), BF),
            pltpu.VMEM((head, keys), BF),
            pltpu.VMEM((width, tile), BF),
            pltpu.VMEM((keys, tile), F32),
        ],
        compiler_params=params(40),
        cost_estimate=cost(8 * tile * keys * width, 2 * (4 * tile * width + 2 * keys * head)),
        name="forward",
    )(info, q, kv_self, kv_anc)


def masked_rows(g_ref, att_ref, at, cols, row_ok):
    g = jnp.where(row_ok, g_ref[at, cols], jnp.zeros((), BF))
    return g, jnp.sum(g.astype(F32) * att_ref[at, cols], axis=1, keepdims=True)


def terms_kernel(
    info_ref, q_ref, g_ref, att_ref, log_ref, anc_ref,
    term_ref,
    k_ref, v_ref, qt_ref, gm_ref, gt_ref, stat_ref, dk_ref, dv_ref,
):
    tile, width = q_ref.shape
    head = k_ref.shape[1]
    heads = width // head
    depth = anc_ref.shape[1]
    root = 1.0 / math.sqrt(head)
    pos = lax.broadcasted_iota(jnp.int32, (tile, 1), 0)
    masked = jnp.where(pos < info_ref[depth], g_ref[...], jnp.zeros((), BF))
    gm_ref[...] = masked
    gt_ref[...] = masked.T
    qt_ref[...] = q_ref[...].T
    for h in range(heads):
        cols = slice(h * head, (h + 1) * head)
        delta = jnp.sum(masked[:, cols].astype(F32) * att_ref[:, cols], axis=1, keepdims=True)
        stat_ref[h : h + 1] = delta.T
    for j in range(depth):
        kv = anc_ref[:, j].reshape(tile, 2 * head)
        rows = slice(j * tile, (j + 1) * tile)
        k_ref[rows] = kv[:, :head]
        v_ref[rows] = kv[:, head:]
    for first in range(0, tile, ROWS):
        at = slice(first, first + ROWS)
        for h in range(heads):
            cols = slice(h * head, (h + 1) * head)
            p = jnp.exp2(nn(k_ref[...], qt_ref[cols, at]) * (LOG2E * root) - log_ref[h : h + 1, at])
            dp = nn(v_ref[...], gt_ref[cols, at])
            ds = (p * (dp - stat_ref[h : h + 1, at])).astype(BF)
            dk, dv = nn(ds, q_ref[at, cols]), nn(p.astype(BF), gm_ref[at, cols])
            if first == 0 and h == 0:
                dk_ref[...] = dk
                dv_ref[...] = dv
            else:
                dk_ref[...] += dk
                dv_ref[...] += dv
    for j in range(depth):
        rows = slice(j * tile, (j + 1) * tile)
        shape = (tile // 16, 16, head)
        visible = pos < info_ref[j]
        term_ref[:, j, :, :head] = jnp.where(visible, dk_ref[rows] * root, 0.0).astype(BF).reshape(shape)
        term_ref[:, j, :, head:] = jnp.where(visible, dv_ref[rows], 0.0).astype(BF).reshape(shape)


def ancestor_terms(info, q, g, att, log_total, kv_anc):
    tile, width = q.shape
    head = kv_anc.shape[3] // 2
    keys = kv_anc.shape[1] * tile
    return pl.pallas_call(
        terms_kernel,
        out_shape=jax.ShapeDtypeStruct(kv_anc.shape, BF),
        in_specs=[SMEM_SPEC] + [VMEM_SPEC] * 5,
        out_specs=VMEM_SPEC,
        scratch_shapes=[
            pltpu.VMEM((keys, head), BF),
            pltpu.VMEM((keys, head), BF),
            pltpu.VMEM((width, tile), BF),
            pltpu.VMEM((tile, width), BF),
            pltpu.VMEM((width, tile), BF),
            pltpu.VMEM((width // head, tile), F32),
            pltpu.VMEM((keys, head), F32),
            pltpu.VMEM((keys, head), F32),
        ],
        compiler_params=params(24),
        cost_estimate=cost(16 * tile * keys * width, 2 * (2 * tile * width + 4 * keys * head)),
        name="ancestor_terms",
    )(info, q, g, att, log_total, kv_anc)


def local_kernel(
    info_ref, q_ref, g_ref, att_ref, log_ref, self_ref, anc_ref,
    dq_ref, own_ref,
    kt_ref, vt_ref, k_ref, bias_ref,
):
    tile, width = q_ref.shape
    head = kt_ref.shape[0]
    heads = width // head
    depth = anc_ref.shape[1]
    length = info_ref[depth]
    load_tiles(self_ref, anc_ref, kt_ref, vt_ref, k_ref)
    fill_bias(info_ref, bias_ref, tile)
    root = 1.0 / math.sqrt(head)
    own_ref[...] = jnp.zeros_like(own_ref)
    log_total = log_ref[...].T
    for first in range(0, tile, ROWS):
        at = slice(first, first + ROWS)
        own = first + ROWS
        keys = depth * tile + own
        row_ok = first + lax.broadcasted_iota(jnp.int32, (ROWS, 1), 0) < length
        for h in range(heads):
            cols = slice(h * head, (h + 1) * head)
            q = q_ref[at, cols]
            g, delta = masked_rows(g_ref, att_ref, at, cols, row_ok)
            s = block_logits(q, kt_ref, bias_ref, first, keys, tile, LOG2E * root)
            p = jnp.exp2(s - log_total[at, h : h + 1])
            dp = nn(g, vt_ref[:, :keys])
            ds = (p * (dp - delta)).astype(BF)
            dq_ref[at, cols] = (nn(ds, k_ref[:keys]) * root).astype(BF)
            own_ref[:own, :head] += tn(ds[:, depth * tile :], q)
            own_ref[:own, head:] += tn(p[:, depth * tile :].astype(BF), g)
    own_ref[:, :head] = own_ref[:, :head] * root


def local_grads(info, q, g, att, log_total, kv_self, kv_anc):
    tile, width = q.shape
    head = kv_self.shape[2] // 2
    keys = (kv_anc.shape[1] + 1) * tile
    return pl.pallas_call(
        local_kernel,
        out_shape=(
            jax.ShapeDtypeStruct((tile, width), BF),
            jax.ShapeDtypeStruct((tile, 2 * head), F32),
        ),
        in_specs=[SMEM_SPEC] + [VMEM_SPEC] * 6,
        out_specs=(VMEM_SPEC,) * 2,
        scratch_shapes=[
            pltpu.VMEM((head, keys), BF),
            pltpu.VMEM((head, keys), BF),
            pltpu.VMEM((keys, head), BF),
            pltpu.VMEM((1, keys), F32),
        ],
        compiler_params=params(24),
        cost_estimate=cost(12 * tile * keys * width, 2 * (3 * tile * width + 4 * keys * head)),
        name="local_grads",
    )(info, q, g, att, log_total, kv_self, kv_anc)


def collect_kernel(table_ref, term_ref, keep_ref, came_ref, out_ref, sum_ref):
    nodes, depth = term_ref.shape[:2]
    width = term_ref.shape[3]
    owner = nodes * depth
    sum_ref[...] = jnp.zeros_like(sum_ref)

    def one_node(n, carry):
        slot = table_ref[owner + n]
        for k in range(depth):
            a = table_ref[n * depth + k]
            target = table_ref[owner + jnp.maximum(a, 0)]
            sum_ref[target] += jnp.where(a >= 0, term_ref[slot, k].astype(F32), 0.0)
        return carry

    lax.fori_loop(0, nodes, one_node, 0, unroll=4)
    out_ref[:, :, :width] = sum_ref[...].astype(BF)
    out_ref[:, :, width:] = (keep_ref[...].astype(F32) + came_ref[...].astype(F32)).astype(BF)


def collect(table, terms, keep, came):
    nodes, chunk, width = terms.shape[0], terms.shape[2], terms.shape[3]
    return pl.pallas_call(
        collect_kernel,
        out_shape=jax.ShapeDtypeStruct((nodes, chunk, width + keep.shape[2]), BF),
        in_specs=[SMEM_SPEC] + [VMEM_SPEC] * 3,
        out_specs=VMEM_SPEC,
        scratch_shapes=[pltpu.VMEM((nodes, chunk, width), F32)],
        compiler_params=params(),
        cost_estimate=cost(0, 4 * terms.size),
        name="collect",
    )(table, terms, keep, came)


def sum_parts_kernel(odd_ref, *refs):
    parts, (keep_ref, send_ref) = refs[:-2], refs[-2:]
    half = keep_ref.shape[2]
    for out_ref, first in ((keep_ref, odd_ref[0] * half), (send_ref, (1 - odd_ref[0]) * half)):
        at = pl.ds(pl.multiple_of(first, half), half)
        total = parts[0][at, :].astype(F32)
        for part in parts[1:]:
            total = total + part[at, :].astype(F32)
        out_ref[...] = total.astype(out_ref.dtype).T.reshape(out_ref.shape)


def sum_parts(odd, parts, nodes):
    width, rows = parts[0].shape
    shape = (nodes, rows // nodes, width // 2)
    return pl.pallas_call(
        sum_parts_kernel,
        out_shape=(jax.ShapeDtypeStruct(shape, BF), jax.ShapeDtypeStruct(shape, BF)),
        in_specs=[SMEM_SPEC] + [VMEM_SPEC] * len(parts),
        out_specs=(VMEM_SPEC, VMEM_SPEC),
        compiler_params=params(12),
        cost_estimate=cost(0, 10 * rows * width),
        name="sum_parts",
    )(odd, *parts)


def finish_kernel(weight_scale, got_ref, own_ref, gk_ref, gv_ref, gw_ref):
    tile, width = own_ref.shape
    head = width // 2
    total = got_ref[:, :, :width].reshape(tile, width).astype(F32) + own_ref[...]
    gk_ref[...] = total[:, :head].astype(BF)
    gv_ref[...] = total[:, head:].astype(BF)
    nodes, rows, half = got_ref.shape[0], got_ref.shape[1], got_ref.shape[2] - width
    sent = got_ref[:, :, width:].astype(F32).reshape(nodes // 2, 2, rows, half)
    sums = jnp.sum(sent, axis=0) * weight_scale
    gw_ref[:, :half] = sums[0]
    gw_ref[:, half:] = sums[1]


def finish(got, own, weight_scale):
    tile, width = own.shape
    return pl.pallas_call(
        lambda *refs: finish_kernel(weight_scale, *refs),
        out_shape=(
            jax.ShapeDtypeStruct((tile, width // 2), BF),
            jax.ShapeDtypeStruct((tile, width // 2), BF),
            jax.ShapeDtypeStruct((got.shape[1], 2 * (got.shape[2] - width)), F32),
        ),
        in_specs=[VMEM_SPEC] * 2,
        out_specs=(VMEM_SPEC,) * 3,
        compiler_params=params(),
        cost_estimate=cost(0, 4 * got.size),
        name="finish",
    )(got, own)


def ring(size, step):
    return [(i, (i + step) % size) for i in range(size)]


def per_device(queries, keys, values, grad_out, out_weight, ancestors, owner, lengths):
    q = queries[0, 0]
    tile, width = q.shape
    head = keys.shape[-1]
    seq = ("z", "y")
    nodes = lax.axis_size(seq)
    xs = lax.axis_size("x")
    core = lax.axis_index("core")
    x = lax.axis_index("x")
    me = lax.axis_index(seq).astype(jnp.int32).reshape(1)

    table = join_tables(ancestors[0], owner[0], lengths[0], me)
    kv_self = join(keys[0, 0], values[0, 0])
    kv_self, out_weight = lax.optimization_barrier((kv_self, out_weight))
    chunks = lax.all_to_all(kv_self, seq, 0, 0, tiled=True)
    def along(rows, step):
        return lax.ppermute(rows, "x", ring(xs, step))

    below, above = along(out_weight, 1), along(out_weight, xs - 1)
    mid = out_weight.shape[0] // 2
    below_low, above_high = below[:mid], above[mid:]
    grads = grad_out[0, 0]
    place = jnp.stack([x, core]).astype(jnp.int32)
    other = other_half(place, grads, xs)
    chunks, other, below, above, below_low, above_high = lax.optimization_barrier(
        (chunks, other, below, above, below_low, above_high)
    )
    weight = [[out_weight], [below], [along(below_low, 1), along(above_high, xs - 1)], [above]]
    sibling = lax.ppermute(other, "core", ring(2, 1))
    routed, info = route(table, chunks, ancestors.shape[2])
    kv_anc = lax.all_to_all(routed, seq, 0, 0, tiled=True)

    blocks = []
    for block in weight:
        blocks += [block, [lax.ppermute(rows, "core", ring(2, 1)) for rows in block]]
    grad_att = grad_attention(place, grads, blocks)

    att, att_low, log_total = forward(info, q, kv_self, kv_anc)
    att_sibling = lax.ppermute(att_low, "core", ring(2, 1))
    terms = ancestor_terms(info, q, grad_att, att, log_total, kv_anc)

    pieces = make_pieces(place, xs, grads, sibling, att_low, att_sibling)
    terms, pieces = lax.optimization_barrier((terms, pieces))
    own_piece, up, opposite_low, opposite_high, down = pieces
    from_below, from_above = along(opposite_low, 1), along(opposite_high, xs - 1)
    up, down = fold(up, from_below, down, from_above)
    parts = [own_piece, along(up, 1), along(down, xs - 1)]
    terms = lax.all_to_all(terms, seq, 0, 0, tiled=True)
    odd = lax.rem(lax.axis_index("y"), 2).astype(jnp.int32).reshape(1)
    grad_q, own = local_grads(info, q, grad_att, att, log_total, kv_self, kv_anc)
    keep, send = sum_parts(odd, parts, nodes)
    grad_q, own, send = lax.optimization_barrier((grad_q, own, send))
    came = lax.ppermute(send, "y", [(i, i ^ 1) for i in range(lax.axis_size("y"))])
    got = lax.all_to_all(collect(table, terms, keep, came), seq, 0, 0, tiled=True)
    token_count = 2 * xs * nodes * tile
    grad_k, grad_v, grad_w = finish(got, own, 1.0 / math.sqrt(token_count))
    return grad_q[None, None], grad_k[None, None], grad_v[None, None], grad_w


def solution(mesh):
    dp, seq = mesh.devices.shape
    fine = Mesh(mesh.devices.reshape(dp // 2, 2, seq // 4, 4), ("x", "core", "z", "y"))
    d, s = ("x", "core"), ("z", "y")
    placed = (
        P(d, s, None, None),
        P(d, s, None, None),
        P(d, s, None, None),
        P(d, s, None, None),
        P(d, None),
        P(d, None, None),
        P(d, None),
        P(d, None),
    )
    return jax.shard_map(
        per_device,
        mesh=fine,
        in_specs=placed,
        out_specs=(
            P(d, s, None, None),
            P(d, s, None, None),
            P(d, s, None, None),
            P(d + s, None),
        ),
        check_vma=False,
    )
```

```python
import math

import jax
import jax.numpy as jnp
from jax import lax
from jax.experimental import pallas as pl
from jax.experimental.pallas import tpu as pltpu
from jax.sharding import Mesh, PartitionSpec as P

BF = jnp.bfloat16
F32 = jnp.float32
MASKED = -1e30
LOG2E = 1.0 / math.log(2.0)
MIB = 1024 * 1024
VMEM_MIB = 8
SMEM_SPEC = pl.BlockSpec(memory_space=pltpu.SMEM)
VMEM_SPEC = pl.BlockSpec(memory_space=pltpu.VMEM)
HBM_SPEC = pl.BlockSpec(memory_space=pltpu.HBM)
ROWS = 256


def nn(a, b):
    return lax.dot_general(a, b, (((1,), (0,)), ((), ())), preferred_element_type=F32)


def tn(a, b):
    return lax.dot_general(a, b, (((0,), (0,)), ((), ())), preferred_element_type=F32)


def params(mib=VMEM_MIB):
    return pltpu.CompilerParams(vmem_limit_bytes=mib * MIB)


def cost(flops, moved):
    return pl.CostEstimate(flops=int(flops), bytes_accessed=int(moved), transcendentals=0)


def long_cost():
    return cost(10**13, 10**11)


def join_kernel(k_ref, v_ref, out_ref):
    head = k_ref.shape[2]
    out_ref[:, :, :head] = k_ref[...]
    out_ref[:, :, head:] = v_ref[...]


def join(k, v):
    tile, head = k.shape
    shape = (tile // 16, 16, head)
    return pl.pallas_call(
        join_kernel,
        out_shape=jax.ShapeDtypeStruct((tile // 16, 16, 2 * head), BF),
        in_specs=[VMEM_SPEC] * 2,
        out_specs=VMEM_SPEC,
        compiler_params=params(56),
        cost_estimate=cost(0, 8 * k.size),
        name="join",
    )(k.reshape(shape), v.reshape(shape))


def halves_kernel(place_ref, in_ref, out_ref):
    out_ref[...] = in_ref[...]


def other_half(place, grads, xs):
    tile, features = grads.shape
    block = features // (2 * xs)
    return pl.pallas_call(
        halves_kernel,
        grid_spec=pltpu.PrefetchScalarGridSpec(
            num_scalar_prefetch=1,
            grid=(xs,),
            in_specs=[pl.BlockSpec((tile, block), lambda i, place: (0, 2 * i + 1 - place[1]))],
            out_specs=pl.BlockSpec((tile, block), lambda i, place: (0, i)),
        ),
        out_shape=jax.ShapeDtypeStruct((tile, features // 2), BF),
        compiler_params=params(),
        cost_estimate=long_cost(),
        name="other_half",
    )(place, grads)


def grad_attention_kernel(runs, place_ref, grads_ref, *refs):
    count = sum(runs)
    refs, (out_ref, grads_stage, weight_stage, sems) = refs[:count], refs[count:]
    rows_each = weight_stage.shape[1]
    xs = len(runs) // 2
    blocks, refs = [], list(refs)
    for i, run in enumerate(runs):
        source = 2 * lax.rem(place_ref[0] + xs - i // 2, xs) + lax.rem(place_ref[1] + i % 2, 2)
        at = pl.ds(pl.multiple_of(source * rows_each, rows_each), rows_each)
        loads = [pltpu.make_async_copy(grads_ref.at[:, at], grads_stage.at[i], sems.at[i, 0])]
        first = 0
        for part, rows in enumerate(refs[:run]):
            to = weight_stage.at[i, pl.ds(first, rows.shape[0])]
            loads.append(pltpu.make_async_copy(rows, to, sems.at[i, 1 + part]))
            first += rows.shape[0]
        refs = refs[run:]
        for load in loads:
            load.start()
        blocks.append(loads)
    total = 0.0
    for i, loads in enumerate(blocks):
        for load in loads:
            load.wait()
        total = total + nn(grads_stage[i], weight_stage[i])
    out_ref[...] = total.astype(BF)


def grad_attention(place, grads, blocks):
    tile, features = grads.shape
    runs = [rows for block in blocks for rows in block]
    width = runs[0].shape[1]
    each = features // len(blocks)
    return pl.pallas_call(
        lambda *refs: grad_attention_kernel([len(block) for block in blocks], *refs),
        out_shape=jax.ShapeDtypeStruct((tile, width), BF),
        in_specs=[SMEM_SPEC] + [HBM_SPEC] * (1 + len(runs)),
        out_specs=VMEM_SPEC,
        scratch_shapes=[
            pltpu.VMEM((len(blocks), tile, each), BF),
            pltpu.VMEM((len(blocks), each, width), BF),
            pltpu.SemaphoreType.DMA((len(blocks), 3)),
        ],
        compiler_params=params(56),
        cost_estimate=cost(2 * tile * features * width, 2 * (tile + width) * features),
        name="grad_attention",
    )(place, grads, *runs)


def pieces_kernel(
    place_ref, grads_ref, sibling_ref, att_ref, att_sibling_ref,
    own_ref, near_ref, opposite_low_ref, opposite_high_ref,
):
    width, block = own_ref.shape
    xs = sibling_ref.shape[1] // block
    mine_t, sibling_t = att_ref[...].T, att_sibling_ref[...].T
    outs = ([own_ref], [near_ref.at[0]], [opposite_low_ref, opposite_high_ref], [near_ref.at[1]])
    for k in (2, 1, 3, 0):
        at = lax.rem(place_ref[0] + k, xs)
        mine = grads_ref[:, pl.ds(pl.multiple_of((2 * at + place_ref[1]) * block, block), block)]
        sibling = sibling_ref[:, pl.ds(pl.multiple_of(at * block, block), block)]
        total = (nn(mine_t, mine) + nn(sibling_t, sibling)).astype(BF)
        first = 0
        for out_ref in outs[k]:
            out_ref[...] = total[first : first + out_ref.shape[0]]
            first += out_ref.shape[0]


def make_pieces(place, xs, grads, sibling, att, att_sibling):
    tile, features = grads.shape
    block = features // (2 * xs)
    width = att.shape[1]
    whole = jax.ShapeDtypeStruct((width, block), BF)
    near = jax.ShapeDtypeStruct((2, width, block), BF)
    half = jax.ShapeDtypeStruct((width // 2, block), BF)
    return pl.pallas_call(
        pieces_kernel,
        out_shape=(whole, near, half, half),
        in_specs=[SMEM_SPEC] + [VMEM_SPEC] * 4,
        out_specs=(VMEM_SPEC,) * 4,
        compiler_params=params(24),
        cost_estimate=cost(4 * tile * block * width * xs, 2 * xs * (2 * tile * block + block * width)),
        name="pieces",
    )(place, grads, sibling, att, att_sibling)


def fold_kernel(near_ref, from_below_ref, from_above_ref, up_out_ref, down_out_ref):
    half = from_below_ref.shape[0]

    def add(a, b):
        return (a.astype(F32) + b.astype(F32)).astype(BF)

    up_out_ref[:half] = add(near_ref[0, :half], from_below_ref[...])
    up_out_ref[half:] = near_ref[0, half:]
    down_out_ref[:half] = near_ref[1, :half]
    down_out_ref[half:] = add(near_ref[1, half:], from_above_ref[...])


def fold(near, from_below, from_above):
    shape = jax.ShapeDtypeStruct(near.shape[1:], BF)
    return pl.pallas_call(
        fold_kernel,
        out_shape=(shape, shape),
        in_specs=[VMEM_SPEC] * 3,
        out_specs=(VMEM_SPEC, VMEM_SPEC),
        compiler_params=params(),
        cost_estimate=long_cost(),
        name="fold",
    )(near, from_below, from_above)


def join_tables(anc, owner, lengths, me):
    return jnp.concatenate([anc.reshape(-1), owner, lengths, me])


def route_kernel(table_ref, chunk_ref, out_ref, info_ref):
    nodes, depth = out_ref.shape[:2]
    owner, lengths = nodes * depth, nodes * (depth + 1)
    me = table_ref[nodes * (depth + 2)]
    zero = jnp.zeros(out_ref.shape[2:], out_ref.dtype)

    def one_node(n, mine):
        slot = table_ref[owner + n]
        for k in range(depth):
            a = table_ref[n * depth + k]
            source = table_ref[owner + jnp.maximum(a, 0)]
            out_ref[slot, k] = jnp.where(a >= 0, chunk_ref[source], zero)
        return jnp.where(slot == me, n, mine)

    mine = lax.fori_loop(0, nodes, one_node, 0, unroll=4)
    for k in range(depth):
        a = table_ref[mine * depth + k]
        info_ref[k] = jnp.where(a >= 0, table_ref[lengths + jnp.maximum(a, 0)], 0)
    info_ref[depth] = table_ref[lengths + mine]


def route(table, chunks, depth):
    nodes = chunks.shape[0]
    return pl.pallas_call(
        route_kernel,
        out_shape=(
            jax.ShapeDtypeStruct((nodes, depth) + chunks.shape[1:], BF),
            jax.ShapeDtypeStruct((depth + 1,), jnp.int32),
        ),
        in_specs=[SMEM_SPEC, VMEM_SPEC],
        out_specs=(VMEM_SPEC, SMEM_SPEC),
        compiler_params=params(),
        cost_estimate=long_cost(),
        name="route",
    )(table, chunks)


def load_tiles(self_ref, anc_ref, kt_ref, vt_ref, k_ref):
    head = kt_ref.shape[0]
    depth = anc_ref.shape[1]
    tile = anc_ref.shape[0] * anc_ref.shape[2]
    for j in range(depth + 1):
        kv = (anc_ref[:, j] if j < depth else self_ref[...]).reshape(tile, 2 * head)
        k_part, v_part = kv[:, :head], kv[:, head:]
        at = slice(j * tile, (j + 1) * tile)
        kt_ref[:, at] = k_part.T
        vt_ref[:, at] = v_part.T
        k_ref[at] = k_part


def fill_bias(info_ref, bias_ref, tile):
    tiles = bias_ref.shape[1] // tile
    pos = lax.broadcasted_iota(jnp.int32, (1, tile), 1)
    for j in range(tiles):
        bias_ref[:, j * tile : (j + 1) * tile] = jnp.where(pos < info_ref[j], 0.0, MASKED)


def block_logits(q, kt_ref, bias_ref, first, width, tile, scale):
    s = nn(q, kt_ref[:, :width]) * scale + bias_ref[:, :width]
    base = kt_ref.shape[1] - tile + first
    q_pos = lax.broadcasted_iota(jnp.int32, (ROWS, ROWS), 0)
    k_pos = lax.broadcasted_iota(jnp.int32, (ROWS, ROWS), 1)
    diagonal = jnp.where(k_pos <= q_pos, s[:, base : base + ROWS], MASKED)
    return jnp.concatenate([s[:, :base], diagonal], axis=1)


def forward_kernel(
    info_ref, q_ref, self_ref, anc_ref, att_ref, low_ref, log_ref, k_ref, vt_ref, qt_ref, bias_ref
):
    tile, width = q_ref.shape
    head = vt_ref.shape[0]
    depth = anc_ref.shape[1]
    scale = LOG2E / math.sqrt(head)
    qt_ref[...] = q_ref[...].T
    pos = lax.broadcasted_iota(jnp.int32, (tile, tile), 0)
    for j in range(depth + 1):
        kv = (anc_ref[:, j] if j < depth else self_ref[...]).reshape(tile, 2 * head)
        rows = slice(j * tile, (j + 1) * tile)
        k_ref[rows] = kv[:, :head]
        vt_ref[:, rows] = kv[:, head:].T
        visible = pos < info_ref[j]
        if j == depth:
            visible = visible & (pos <= lax.broadcasted_iota(jnp.int32, (tile, tile), 1))
        bias_ref[rows] = jnp.where(visible, 0.0, MASKED)
    row_ok = lax.broadcasted_iota(jnp.int32, (tile, 1), 0) < info_ref[depth]
    for h in range(width // head):
        cols = slice(h * head, (h + 1) * head)
        s = nn(k_ref[...], qt_ref[cols]) * scale + bias_ref[...]
        top = jnp.max(s, axis=0, keepdims=True)
        w = jnp.exp2(s - top)
        total = jnp.sum(w, axis=0, keepdims=True)
        att = (nn(vt_ref[...], w.astype(BF)) / total).T
        att_ref[:, cols] = att
        low_ref[:, cols] = jnp.where(row_ok, att, 0.0).astype(BF)
        log_ref[h : h + 1] = top + jnp.log2(total)


def forward(info, q, kv_self, kv_anc):
    tile, width = q.shape
    head = kv_self.shape[2] // 2
    keys = (kv_anc.shape[1] + 1) * tile
    return pl.pallas_call(
        forward_kernel,
        out_shape=(
            jax.ShapeDtypeStruct((tile, width), F32),
            jax.ShapeDtypeStruct((tile, width), BF),
            jax.ShapeDtypeStruct((width // head, tile), F32),
        ),
        in_specs=[SMEM_SPEC] + [VMEM_SPEC] * 3,
        out_specs=(VMEM_SPEC,) * 3,
        scratch_shapes=[
            pltpu.VMEM((keys, head), BF),
            pltpu.VMEM((head, keys), BF),
            pltpu.VMEM((width, tile), BF),
            pltpu.VMEM((keys, tile), F32),
        ],
        compiler_params=params(40),
        cost_estimate=cost(8 * tile * keys * width, 2 * (4 * tile * width + 2 * keys * head)),
        name="forward",
    )(info, q, kv_self, kv_anc)


def masked_rows(g_ref, att_ref, at, cols, row_ok):
    g = jnp.where(row_ok, g_ref[at, cols], jnp.zeros((), BF))
    return g, jnp.sum(g.astype(F32) * att_ref[at, cols], axis=1, keepdims=True)


def terms_kernel(
    info_ref, q_ref, g_ref, att_ref, log_ref, anc_ref,
    term_ref,
    k_ref, v_ref, qt_ref, gm_ref, gt_ref, stat_ref, dk_ref, dv_ref,
):
    tile, width = q_ref.shape
    head = k_ref.shape[1]
    heads = width // head
    depth = anc_ref.shape[1]
    root = 1.0 / math.sqrt(head)
    pos = lax.broadcasted_iota(jnp.int32, (tile, 1), 0)
    masked = jnp.where(pos < info_ref[depth], g_ref[...], jnp.zeros((), BF))
    gm_ref[...] = masked
    gt_ref[...] = masked.T
    qt_ref[...] = q_ref[...].T
    for h in range(heads):
        cols = slice(h * head, (h + 1) * head)
        delta = jnp.sum(masked[:, cols].astype(F32) * att_ref[:, cols], axis=1, keepdims=True)
        stat_ref[h : h + 1] = delta.T
    for j in range(depth):
        kv = anc_ref[:, j].reshape(tile, 2 * head)
        rows = slice(j * tile, (j + 1) * tile)
        k_ref[rows] = kv[:, :head]
        v_ref[rows] = kv[:, head:]
    for first in range(0, tile, ROWS):
        at = slice(first, first + ROWS)
        for h in range(heads):
            cols = slice(h * head, (h + 1) * head)
            p = jnp.exp2(nn(k_ref[...], qt_ref[cols, at]) * (LOG2E * root) - log_ref[h : h + 1, at])
            dp = nn(v_ref[...], gt_ref[cols, at])
            ds = (p * (dp - stat_ref[h : h + 1, at])).astype(BF)
            dk, dv = nn(ds, q_ref[at, cols]), nn(p.astype(BF), gm_ref[at, cols])
            if first == 0 and h == 0:
                dk_ref[...] = dk
                dv_ref[...] = dv
            else:
                dk_ref[...] += dk
                dv_ref[...] += dv
    for j in range(depth):
        rows = slice(j * tile, (j + 1) * tile)
        shape = (tile // 16, 16, head)
        visible = pos < info_ref[j]
        term_ref[:, j, :, :head] = jnp.where(visible, dk_ref[rows] * root, 0.0).astype(BF).reshape(shape)
        term_ref[:, j, :, head:] = jnp.where(visible, dv_ref[rows], 0.0).astype(BF).reshape(shape)


def ancestor_terms(info, q, g, att, log_total, kv_anc):
    tile, width = q.shape
    head = kv_anc.shape[3] // 2
    keys = kv_anc.shape[1] * tile
    return pl.pallas_call(
        terms_kernel,
        out_shape=jax.ShapeDtypeStruct(kv_anc.shape, BF),
        in_specs=[SMEM_SPEC] + [VMEM_SPEC] * 5,
        out_specs=VMEM_SPEC,
        scratch_shapes=[
            pltpu.VMEM((keys, head), BF),
            pltpu.VMEM((keys, head), BF),
            pltpu.VMEM((width, tile), BF),
            pltpu.VMEM((tile, width), BF),
            pltpu.VMEM((width, tile), BF),
            pltpu.VMEM((width // head, tile), F32),
            pltpu.VMEM((keys, head), F32),
            pltpu.VMEM((keys, head), F32),
        ],
        compiler_params=params(24),
        cost_estimate=cost(16 * tile * keys * width, 2 * (2 * tile * width + 4 * keys * head)),
        name="ancestor_terms",
    )(info, q, g, att, log_total, kv_anc)


def local_kernel(
    info_ref, q_ref, g_ref, att_ref, log_ref, self_ref, anc_ref,
    dq_ref, own_ref,
    kt_ref, vt_ref, k_ref, bias_ref,
):
    tile, width = q_ref.shape
    head = kt_ref.shape[0]
    heads = width // head
    depth = anc_ref.shape[1]
    length = info_ref[depth]
    load_tiles(self_ref, anc_ref, kt_ref, vt_ref, k_ref)
    fill_bias(info_ref, bias_ref, tile)
    root = 1.0 / math.sqrt(head)
    own_ref[...] = jnp.zeros_like(own_ref)
    log_total = log_ref[...].T
    for first in range(0, tile, ROWS):
        at = slice(first, first + ROWS)
        own = first + ROWS
        keys = depth * tile + own
        row_ok = first + lax.broadcasted_iota(jnp.int32, (ROWS, 1), 0) < length
        for h in range(heads):
            cols = slice(h * head, (h + 1) * head)
            q = q_ref[at, cols]
            g, delta = masked_rows(g_ref, att_ref, at, cols, row_ok)
            s = block_logits(q, kt_ref, bias_ref, first, keys, tile, LOG2E * root)
            p = jnp.exp2(s - log_total[at, h : h + 1])
            dp = nn(g, vt_ref[:, :keys])
            ds = (p * (dp - delta)).astype(BF)
            dq_ref[at, cols] = (nn(ds, k_ref[:keys]) * root).astype(BF)
            own_ref[:own, :head] += tn(ds[:, depth * tile :], q)
            own_ref[:own, head:] += tn(p[:, depth * tile :].astype(BF), g)
    own_ref[:, :head] = own_ref[:, :head] * root


def local_grads(info, q, g, att, log_total, kv_self, kv_anc):
    tile, width = q.shape
    head = kv_self.shape[2] // 2
    keys = (kv_anc.shape[1] + 1) * tile
    return pl.pallas_call(
        local_kernel,
        out_shape=(
            jax.ShapeDtypeStruct((tile, width), BF),
            jax.ShapeDtypeStruct((tile, 2 * head), F32),
        ),
        in_specs=[SMEM_SPEC] + [VMEM_SPEC] * 6,
        out_specs=(VMEM_SPEC,) * 2,
        scratch_shapes=[
            pltpu.VMEM((head, keys), BF),
            pltpu.VMEM((head, keys), BF),
            pltpu.VMEM((keys, head), BF),
            pltpu.VMEM((1, keys), F32),
        ],
        compiler_params=params(24),
        cost_estimate=cost(12 * tile * keys * width, 2 * (3 * tile * width + 4 * keys * head)),
        name="local_grads",
    )(info, q, g, att, log_total, kv_self, kv_anc)


def collect_kernel(table_ref, term_ref, keep_ref, came_ref, out_ref, sum_ref):
    nodes, depth = term_ref.shape[:2]
    width = term_ref.shape[3]
    owner = nodes * depth
    sum_ref[...] = jnp.zeros_like(sum_ref)

    def one_node(n, carry):
        slot = table_ref[owner + n]
        for k in range(depth):
            a = table_ref[n * depth + k]
            target = table_ref[owner + jnp.maximum(a, 0)]
            sum_ref[target] += jnp.where(a >= 0, term_ref[slot, k].astype(F32), 0.0)
        return carry

    lax.fori_loop(0, nodes, one_node, 0, unroll=4)
    out_ref[:, :, :width] = sum_ref[...].astype(BF)
    out_ref[:, :, width:] = (keep_ref[...].astype(F32) + came_ref[...].astype(F32)).astype(BF)


def collect(table, terms, keep, came):
    nodes, chunk, width = terms.shape[0], terms.shape[2], terms.shape[3]
    return pl.pallas_call(
        collect_kernel,
        out_shape=jax.ShapeDtypeStruct((nodes, chunk, width + keep.shape[2]), BF),
        in_specs=[SMEM_SPEC] + [VMEM_SPEC] * 3,
        out_specs=VMEM_SPEC,
        scratch_shapes=[pltpu.VMEM((nodes, chunk, width), F32)],
        compiler_params=params(),
        cost_estimate=cost(0, 4 * terms.size),
        name="collect",
    )(table, terms, keep, came)


def sum_parts_kernel(odd_ref, *refs):
    parts, (keep_ref, send_ref) = refs[:-2], refs[-2:]
    half = keep_ref.shape[2]
    for out_ref, first in ((keep_ref, odd_ref[0] * half), (send_ref, (1 - odd_ref[0]) * half)):
        at = pl.ds(pl.multiple_of(first, half), half)
        total = parts[0][at, :].astype(F32)
        for part in parts[1:]:
            total = total + part[at, :].astype(F32)
        out_ref[...] = total.astype(out_ref.dtype).T.reshape(out_ref.shape)


def sum_parts(odd, parts, nodes):
    width, rows = parts[0].shape
    shape = (nodes, rows // nodes, width // 2)
    return pl.pallas_call(
        sum_parts_kernel,
        out_shape=(jax.ShapeDtypeStruct(shape, BF), jax.ShapeDtypeStruct(shape, BF)),
        in_specs=[SMEM_SPEC] + [VMEM_SPEC] * len(parts),
        out_specs=(VMEM_SPEC, VMEM_SPEC),
        compiler_params=params(12),
        cost_estimate=cost(0, 10 * rows * width),
        name="sum_parts",
    )(odd, *parts)


def finish_kernel(weight_scale, got_ref, own_ref, gk_ref, gv_ref, gw_ref):
    tile, width = own_ref.shape
    head = width // 2
    total = got_ref[:, :, :width].reshape(tile, width).astype(F32) + own_ref[...]
    gk_ref[...] = total[:, :head].astype(BF)
    gv_ref[...] = total[:, head:].astype(BF)
    nodes, rows, half = got_ref.shape[0], got_ref.shape[1], got_ref.shape[2] - width
    sent = got_ref[:, :, width:].astype(F32).reshape(nodes // 2, 2, rows, half)
    sums = jnp.sum(sent, axis=0) * weight_scale
    gw_ref[:, :half] = sums[0]
    gw_ref[:, half:] = sums[1]


def finish(got, own, weight_scale):
    tile, width = own.shape
    return pl.pallas_call(
        lambda *refs: finish_kernel(weight_scale, *refs),
        out_shape=(
            jax.ShapeDtypeStruct((tile, width // 2), BF),
            jax.ShapeDtypeStruct((tile, width // 2), BF),
            jax.ShapeDtypeStruct((got.shape[1], 2 * (got.shape[2] - width)), F32),
        ),
        in_specs=[VMEM_SPEC] * 2,
        out_specs=(VMEM_SPEC,) * 3,
        compiler_params=params(),
        cost_estimate=cost(0, 4 * got.size),
        name="finish",
    )(got, own)


def ring(size, step):
    return [(i, (i + step) % size) for i in range(size)]


def per_device(queries, keys, values, grad_out, out_weight, ancestors, owner, lengths):
    q = queries[0, 0]
    tile, width = q.shape
    head = keys.shape[-1]
    seq = ("z", "y")
    nodes = lax.axis_size(seq)
    xs = lax.axis_size("x")
    core = lax.axis_index("core")
    x = lax.axis_index("x")
    me = lax.axis_index(seq).astype(jnp.int32).reshape(1)

    table = join_tables(ancestors[0], owner[0], lengths[0], me)
    kv_self = join(keys[0, 0], values[0, 0])
    kv_self, out_weight = lax.optimization_barrier((kv_self, out_weight))
    chunks = lax.all_to_all(kv_self, seq, 0, 0, tiled=True)
    def along(rows, step):
        return lax.ppermute(rows, "x", ring(xs, step))

    below, above = along(out_weight, 1), along(out_weight, xs - 1)
    mid = out_weight.shape[0] // 2
    below_low, above_high = below[:mid], above[mid:]
    grads = grad_out[0, 0]
    place = jnp.stack([x, core]).astype(jnp.int32)
    other = other_half(place, grads, xs)
    chunks, other, below, above, below_low, above_high = lax.optimization_barrier(
        (chunks, other, below, above, below_low, above_high)
    )
    weight = [[out_weight], [below], [along(below_low, 1), along(above_high, xs - 1)], [above]]
    sibling = lax.ppermute(other, "core", ring(2, 1))
    routed, info = route(table, chunks, ancestors.shape[2])
    kv_anc = lax.all_to_all(routed, seq, 0, 0, tiled=True)

    blocks = []
    for block in weight:
        blocks += [block, [lax.ppermute(rows, "core", ring(2, 1)) for rows in block]]
    grad_att = grad_attention(place, grads, blocks)

    att, att_low, log_total = forward(info, q, kv_self, kv_anc)
    att_sibling = lax.ppermute(att_low, "core", ring(2, 1))
    terms = ancestor_terms(info, q, grad_att, att, log_total, kv_anc)

    pieces = make_pieces(place, xs, grads, sibling, att_low, att_sibling)
    terms, pieces = lax.optimization_barrier((terms, pieces))
    own_piece, near, opposite_low, opposite_high = pieces
    from_below, from_above = along(opposite_low, 1), along(opposite_high, xs - 1)
    up, down = fold(near, from_below, from_above)
    parts = [own_piece, along(up, 1), along(down, xs - 1)]
    terms = lax.all_to_all(terms, seq, 0, 0, tiled=True)
    odd = lax.rem(lax.axis_index("y"), 2).astype(jnp.int32).reshape(1)
    grad_q, own = local_grads(info, q, grad_att, att, log_total, kv_self, kv_anc)
    keep, send = sum_parts(odd, parts, nodes)
    grad_q, own, send = lax.optimization_barrier((grad_q, own, send))
    came = lax.ppermute(send, "y", [(i, i ^ 1) for i in range(lax.axis_size("y"))])
    got = lax.all_to_all(collect(table, terms, keep, came), seq, 0, 0, tiled=True)
    token_count = 2 * xs * nodes * tile
    grad_k, grad_v, grad_w = finish(got, own, 1.0 / math.sqrt(token_count))
    return grad_q[None, None], grad_k[None, None], grad_v[None, None], grad_w


def solution(mesh):
    dp, seq = mesh.devices.shape
    fine = Mesh(mesh.devices.reshape(dp // 2, 2, seq // 4, 4), ("x", "core", "z", "y"))
    d, s = ("x", "core"), ("z", "y")
    placed = (
        P(d, s, None, None),
        P(d, s, None, None),
        P(d, s, None, None),
        P(d, s, None, None),
        P(d, None),
        P(d, None, None),
        P(d, None),
        P(d, None),
    )
    return jax.shard_map(
        per_device,
        mesh=fine,
        in_specs=placed,
        out_specs=(
            P(d, s, None, None),
            P(d, s, None, None),
            P(d, s, None, None),
            P(d + s, None),
        ),
        check_vma=False,
    )
```

```python
import math

import jax
import jax.numpy as jnp
from jax import lax
from jax.experimental import pallas as pl
from jax.experimental.pallas import tpu as pltpu
from jax.sharding import Mesh, PartitionSpec as P

BF = jnp.bfloat16
F32 = jnp.float32
MASKED = -1e30
LOG2E = 1.0 / math.log(2.0)
MIB = 1024 * 1024
VMEM_MIB = 8
SMEM_SPEC = pl.BlockSpec(memory_space=pltpu.SMEM)
VMEM_SPEC = pl.BlockSpec(memory_space=pltpu.VMEM)
HBM_SPEC = pl.BlockSpec(memory_space=pltpu.HBM)
ROWS = 256


def nn(a, b):
    return lax.dot_general(a, b, (((1,), (0,)), ((), ())), preferred_element_type=F32)


def tn(a, b):
    return lax.dot_general(a, b, (((0,), (0,)), ((), ())), preferred_element_type=F32)


def params(mib=VMEM_MIB):
    return pltpu.CompilerParams(vmem_limit_bytes=mib * MIB)


def cost(flops, moved):
    return pl.CostEstimate(flops=int(flops), bytes_accessed=int(moved), transcendentals=0)


def long_cost():
    return cost(10**13, 10**11)


def join_kernel(k_ref, v_ref, out_ref):
    head = k_ref.shape[2]
    out_ref[:, :, :head] = k_ref[...]
    out_ref[:, :, head:] = v_ref[...]


def join(k, v):
    tile, head = k.shape
    shape = (tile // 16, 16, head)
    return pl.pallas_call(
        join_kernel,
        out_shape=jax.ShapeDtypeStruct((tile // 16, 16, 2 * head), BF),
        in_specs=[VMEM_SPEC] * 2,
        out_specs=VMEM_SPEC,
        compiler_params=params(56),
        cost_estimate=cost(0, 8 * k.size),
        name="join",
    )(k.reshape(shape), v.reshape(shape))


def halves_kernel(place_ref, in_ref, out_ref):
    out_ref[...] = in_ref[...]


def other_half(place, grads, xs):
    tile, features = grads.shape
    block = features // (2 * xs)
    return pl.pallas_call(
        halves_kernel,
        grid_spec=pltpu.PrefetchScalarGridSpec(
            num_scalar_prefetch=1,
            grid=(xs,),
            in_specs=[pl.BlockSpec((tile, block), lambda i, place: (0, 2 * i + 1 - place[1]))],
            out_specs=pl.BlockSpec((tile, block), lambda i, place: (0, i)),
        ),
        out_shape=jax.ShapeDtypeStruct((tile, features // 2), BF),
        compiler_params=params(),
        cost_estimate=long_cost(),
        name="other_half",
    )(place, grads)


def grad_attention_kernel(runs, place_ref, grads_ref, *refs):
    count = sum(runs)
    refs, (out_ref, grads_stage, weight_stage, sems) = refs[:count], refs[count:]
    rows_each = weight_stage.shape[1]
    xs = len(runs) // 2
    blocks, refs = [], list(refs)
    for i, run in enumerate(runs):
        source = 2 * lax.rem(place_ref[0] + xs - i // 2, xs) + lax.rem(place_ref[1] + i % 2, 2)
        at = pl.ds(pl.multiple_of(source * rows_each, rows_each), rows_each)
        loads = [pltpu.make_async_copy(grads_ref.at[:, at], grads_stage.at[i], sems.at[i, 0])]
        first = 0
        for part, rows in enumerate(refs[:run]):
            to = weight_stage.at[i, pl.ds(first, rows.shape[0])]
            loads.append(pltpu.make_async_copy(rows, to, sems.at[i, 1 + part]))
            first += rows.shape[0]
        refs = refs[run:]
        for load in loads:
            load.start()
        blocks.append(loads)
    total = 0.0
    for i, loads in enumerate(blocks):
        for load in loads:
            load.wait()
        total = total + nn(grads_stage[i], weight_stage[i])
    out_ref[...] = total.astype(BF)


def grad_attention(place, grads, blocks):
    tile, features = grads.shape
    runs = [rows for block in blocks for rows in block]
    width = runs[0].shape[1]
    each = features // len(blocks)
    return pl.pallas_call(
        lambda *refs: grad_attention_kernel([len(block) for block in blocks], *refs),
        out_shape=jax.ShapeDtypeStruct((tile, width), BF),
        in_specs=[SMEM_SPEC] + [HBM_SPEC] * (1 + len(runs)),
        out_specs=VMEM_SPEC,
        scratch_shapes=[
            pltpu.VMEM((len(blocks), tile, each), BF),
            pltpu.VMEM((len(blocks), each, width), BF),
            pltpu.SemaphoreType.DMA((len(blocks), 3)),
        ],
        compiler_params=params(56),
        cost_estimate=cost(2 * tile * features * width, 2 * (tile + width) * features),
        name="grad_attention",
    )(place, grads, *runs)


def pieces_kernel(
    place_ref, grads_ref, sibling_ref, att_ref, att_sibling_ref,
    own_ref, near_ref, opposite_low_ref, opposite_high_ref,
):
    width, block = own_ref.shape
    xs = sibling_ref.shape[1] // block
    mine_t, sibling_t = att_ref[...].T, att_sibling_ref[...].T
    outs = ([own_ref], [near_ref.at[0]], [opposite_low_ref, opposite_high_ref], [near_ref.at[1]])
    for k in (2, 1, 3, 0):
        at = lax.rem(place_ref[0] + k, xs)
        mine = grads_ref[:, pl.ds(pl.multiple_of((2 * at + place_ref[1]) * block, block), block)]
        sibling = sibling_ref[:, pl.ds(pl.multiple_of(at * block, block), block)]
        total = (nn(mine_t, mine) + nn(sibling_t, sibling)).astype(BF)
        first = 0
        for out_ref in outs[k]:
            out_ref[...] = total[first : first + out_ref.shape[0]]
            first += out_ref.shape[0]


def make_pieces(place, xs, grads, sibling, att, att_sibling):
    tile, features = grads.shape
    block = features // (2 * xs)
    width = att.shape[1]
    whole = jax.ShapeDtypeStruct((width, block), BF)
    near = jax.ShapeDtypeStruct((2, width, block), BF)
    half = jax.ShapeDtypeStruct((width // 2, block), BF)
    return pl.pallas_call(
        pieces_kernel,
        out_shape=(whole, near, half, half),
        in_specs=[SMEM_SPEC] + [VMEM_SPEC] * 4,
        out_specs=(VMEM_SPEC,) * 4,
        compiler_params=params(24),
        cost_estimate=cost(4 * tile * block * width * xs, 2 * xs * (2 * tile * block + block * width)),
        name="pieces",
    )(place, grads, sibling, att, att_sibling)


def fold_kernel(near_ref, from_below_ref, from_above_ref, up_out_ref, down_out_ref):
    half = from_below_ref.shape[0]

    def add(a, b):
        return (a.astype(F32) + b.astype(F32)).astype(BF)

    up_out_ref[:half] = add(near_ref[0, :half], from_below_ref[...])
    up_out_ref[half:] = near_ref[0, half:]
    down_out_ref[:half] = near_ref[1, :half]
    down_out_ref[half:] = add(near_ref[1, half:], from_above_ref[...])


def fold(near, from_below, from_above):
    shape = jax.ShapeDtypeStruct(near.shape[1:], BF)
    return pl.pallas_call(
        fold_kernel,
        out_shape=(shape, shape),
        in_specs=[VMEM_SPEC] * 3,
        out_specs=(VMEM_SPEC, VMEM_SPEC),
        compiler_params=params(),
        cost_estimate=long_cost(),
        name="fold",
    )(near, from_below, from_above)


def join_tables(anc, owner, lengths, me):
    return jnp.concatenate([anc.reshape(-1), owner, lengths, me])


def route_kernel(table_ref, chunk_ref, out_ref, info_ref):
    nodes, depth = out_ref.shape[:2]
    owner, lengths = nodes * depth, nodes * (depth + 1)
    me = table_ref[nodes * (depth + 2)]
    zero = jnp.zeros(out_ref.shape[2:], out_ref.dtype)

    def one_node(n, mine):
        slot = table_ref[owner + n]
        for k in range(depth):
            a = table_ref[n * depth + k]
            source = table_ref[owner + jnp.maximum(a, 0)]
            out_ref[slot, k] = jnp.where(a >= 0, chunk_ref[source], zero)
        return jnp.where(slot == me, n, mine)

    mine = lax.fori_loop(0, nodes, one_node, 0, unroll=16)
    for k in range(depth):
        a = table_ref[mine * depth + k]
        info_ref[k] = jnp.where(a >= 0, table_ref[lengths + jnp.maximum(a, 0)], 0)
    info_ref[depth] = table_ref[lengths + mine]


def route(table, chunks, depth):
    nodes = chunks.shape[0]
    return pl.pallas_call(
        route_kernel,
        out_shape=(
            jax.ShapeDtypeStruct((nodes, depth) + chunks.shape[1:], BF),
            jax.ShapeDtypeStruct((depth + 1,), jnp.int32),
        ),
        in_specs=[SMEM_SPEC, VMEM_SPEC],
        out_specs=(VMEM_SPEC, SMEM_SPEC),
        compiler_params=params(),
        cost_estimate=long_cost(),
        name="route",
    )(table, chunks)


def load_tiles(self_ref, anc_ref, kt_ref, vt_ref, k_ref):
    head = kt_ref.shape[0]
    depth = anc_ref.shape[1]
    tile = anc_ref.shape[0] * anc_ref.shape[2]
    for j in range(depth + 1):
        kv = (anc_ref[:, j] if j < depth else self_ref[...]).reshape(tile, 2 * head)
        k_part, v_part = kv[:, :head], kv[:, head:]
        at = slice(j * tile, (j + 1) * tile)
        kt_ref[:, at] = k_part.T
        vt_ref[:, at] = v_part.T
        k_ref[at] = k_part


def fill_bias(info_ref, bias_ref, tile):
    tiles = bias_ref.shape[1] // tile
    pos = lax.broadcasted_iota(jnp.int32, (1, tile), 1)
    for j in range(tiles):
        bias_ref[:, j * tile : (j + 1) * tile] = jnp.where(pos < info_ref[j], 0.0, MASKED)


def block_logits(q, kt_ref, bias_ref, first, width, tile, scale):
    s = nn(q, kt_ref[:, :width]) * scale + bias_ref[:, :width]
    base = kt_ref.shape[1] - tile + first
    q_pos = lax.broadcasted_iota(jnp.int32, (ROWS, ROWS), 0)
    k_pos = lax.broadcasted_iota(jnp.int32, (ROWS, ROWS), 1)
    diagonal = jnp.where(k_pos <= q_pos, s[:, base : base + ROWS], MASKED)
    return jnp.concatenate([s[:, :base], diagonal], axis=1)


def forward_kernel(
    info_ref, q_ref, self_ref, anc_ref, att_ref, low_ref, log_ref, k_ref, vt_ref, qt_ref, bias_ref
):
    tile, width = q_ref.shape
    head = vt_ref.shape[0]
    depth = anc_ref.shape[1]
    scale = LOG2E / math.sqrt(head)
    qt_ref[...] = q_ref[...].T
    pos = lax.broadcasted_iota(jnp.int32, (tile, tile), 0)
    for j in range(depth + 1):
        kv = (anc_ref[:, j] if j < depth else self_ref[...]).reshape(tile, 2 * head)
        rows = slice(j * tile, (j + 1) * tile)
        k_ref[rows] = kv[:, :head]
        vt_ref[:, rows] = kv[:, head:].T
        visible = pos < info_ref[j]
        if j == depth:
            visible = visible & (pos <= lax.broadcasted_iota(jnp.int32, (tile, tile), 1))
        bias_ref[rows] = jnp.where(visible, 0.0, MASKED)
    row_ok = lax.broadcasted_iota(jnp.int32, (tile, 1), 0) < info_ref[depth]
    for h in range(width // head):
        cols = slice(h * head, (h + 1) * head)
        s = nn(k_ref[...], qt_ref[cols]) * scale + bias_ref[...]
        top = jnp.max(s, axis=0, keepdims=True)
        w = jnp.exp2(s - top)
        total = jnp.sum(w, axis=0, keepdims=True)
        att = (nn(vt_ref[...], w.astype(BF)) / total).T
        att_ref[:, cols] = att
        low_ref[:, cols] = jnp.where(row_ok, att, 0.0).astype(BF)
        log_ref[h : h + 1] = top + jnp.log2(total)


def forward(info, q, kv_self, kv_anc):
    tile, width = q.shape
    head = kv_self.shape[2] // 2
    keys = (kv_anc.shape[1] + 1) * tile
    return pl.pallas_call(
        forward_kernel,
        out_shape=(
            jax.ShapeDtypeStruct((tile, width), F32),
            jax.ShapeDtypeStruct((tile, width), BF),
            jax.ShapeDtypeStruct((width // head, tile), F32),
        ),
        in_specs=[SMEM_SPEC] + [VMEM_SPEC] * 3,
        out_specs=(VMEM_SPEC,) * 3,
        scratch_shapes=[
            pltpu.VMEM((keys, head), BF),
            pltpu.VMEM((head, keys), BF),
            pltpu.VMEM((width, tile), BF),
            pltpu.VMEM((keys, tile), F32),
        ],
        compiler_params=params(40),
        cost_estimate=cost(8 * tile * keys * width, 2 * (4 * tile * width + 2 * keys * head)),
        name="forward",
    )(info, q, kv_self, kv_anc)


def masked_rows(g_ref, att_ref, at, cols, row_ok):
    g = jnp.where(row_ok, g_ref[at, cols], jnp.zeros((), BF))
    return g, jnp.sum(g.astype(F32) * att_ref[at, cols], axis=1, keepdims=True)


def terms_kernel(
    info_ref, q_ref, g_ref, att_ref, log_ref, anc_ref,
    term_ref,
    k_ref, v_ref, qt_ref, gm_ref, gt_ref, stat_ref, dk_ref, dv_ref,
):
    tile, width = q_ref.shape
    head = k_ref.shape[1]
    heads = width // head
    depth = anc_ref.shape[1]
    root = 1.0 / math.sqrt(head)
    pos = lax.broadcasted_iota(jnp.int32, (tile, 1), 0)
    masked = jnp.where(pos < info_ref[depth], g_ref[...], jnp.zeros((), BF))
    gm_ref[...] = masked
    gt_ref[...] = masked.T
    qt_ref[...] = q_ref[...].T
    for h in range(heads):
        cols = slice(h * head, (h + 1) * head)
        delta = jnp.sum(masked[:, cols].astype(F32) * att_ref[:, cols], axis=1, keepdims=True)
        stat_ref[h : h + 1] = delta.T
    for j in range(depth):
        kv = anc_ref[:, j].reshape(tile, 2 * head)
        rows = slice(j * tile, (j + 1) * tile)
        k_ref[rows] = kv[:, :head]
        v_ref[rows] = kv[:, head:]
    for first in range(0, tile, ROWS):
        at = slice(first, first + ROWS)
        for h in range(heads):
            cols = slice(h * head, (h + 1) * head)
            p = jnp.exp2(nn(k_ref[...], qt_ref[cols, at]) * (LOG2E * root) - log_ref[h : h + 1, at])
            dp = nn(v_ref[...], gt_ref[cols, at])
            ds = (p * (dp - stat_ref[h : h + 1, at])).astype(BF)
            dk, dv = nn(ds, q_ref[at, cols]), nn(p.astype(BF), gm_ref[at, cols])
            if first == 0 and h == 0:
                dk_ref[...] = dk
                dv_ref[...] = dv
            else:
                dk_ref[...] += dk
                dv_ref[...] += dv
    for j in range(depth):
        rows = slice(j * tile, (j + 1) * tile)
        shape = (tile // 16, 16, head)
        visible = pos < info_ref[j]
        term_ref[:, j, :, :head] = jnp.where(visible, dk_ref[rows] * root, 0.0).astype(BF).reshape(shape)
        term_ref[:, j, :, head:] = jnp.where(visible, dv_ref[rows], 0.0).astype(BF).reshape(shape)


def ancestor_terms(info, q, g, att, log_total, kv_anc):
    tile, width = q.shape
    head = kv_anc.shape[3] // 2
    keys = kv_anc.shape[1] * tile
    return pl.pallas_call(
        terms_kernel,
        out_shape=jax.ShapeDtypeStruct(kv_anc.shape, BF),
        in_specs=[SMEM_SPEC] + [VMEM_SPEC] * 5,
        out_specs=VMEM_SPEC,
        scratch_shapes=[
            pltpu.VMEM((keys, head), BF),
            pltpu.VMEM((keys, head), BF),
            pltpu.VMEM((width, tile), BF),
            pltpu.VMEM((tile, width), BF),
            pltpu.VMEM((width, tile), BF),
            pltpu.VMEM((width // head, tile), F32),
            pltpu.VMEM((keys, head), F32),
            pltpu.VMEM((keys, head), F32),
        ],
        compiler_params=params(24),
        cost_estimate=cost(16 * tile * keys * width, 2 * (2 * tile * width + 4 * keys * head)),
        name="ancestor_terms",
    )(info, q, g, att, log_total, kv_anc)


def local_kernel(
    info_ref, q_ref, g_ref, att_ref, log_ref, self_ref, anc_ref,
    dq_ref, own_ref,
    kt_ref, vt_ref, k_ref, bias_ref,
):
    tile, width = q_ref.shape
    head = kt_ref.shape[0]
    heads = width // head
    depth = anc_ref.shape[1]
    length = info_ref[depth]
    load_tiles(self_ref, anc_ref, kt_ref, vt_ref, k_ref)
    fill_bias(info_ref, bias_ref, tile)
    root = 1.0 / math.sqrt(head)
    own_ref[...] = jnp.zeros_like(own_ref)
    log_total = log_ref[...].T
    for first in range(0, tile, ROWS):
        at = slice(first, first + ROWS)
        own = first + ROWS
        keys = depth * tile + own
        row_ok = first + lax.broadcasted_iota(jnp.int32, (ROWS, 1), 0) < length
        for h in range(heads):
            cols = slice(h * head, (h + 1) * head)
            q = q_ref[at, cols]
            g, delta = masked_rows(g_ref, att_ref, at, cols, row_ok)
            s = block_logits(q, kt_ref, bias_ref, first, keys, tile, LOG2E * root)
            p = jnp.exp2(s - log_total[at, h : h + 1])
            dp = nn(g, vt_ref[:, :keys])
            ds = (p * (dp - delta)).astype(BF)
            dq_ref[at, cols] = (nn(ds, k_ref[:keys]) * root).astype(BF)
            own_ref[:own, :head] += tn(ds[:, depth * tile :], q)
            own_ref[:own, head:] += tn(p[:, depth * tile :].astype(BF), g)
    own_ref[:, :head] = own_ref[:, :head] * root


def local_grads(info, q, g, att, log_total, kv_self, kv_anc):
    tile, width = q.shape
    head = kv_self.shape[2] // 2
    keys = (kv_anc.shape[1] + 1) * tile
    return pl.pallas_call(
        local_kernel,
        out_shape=(
            jax.ShapeDtypeStruct((tile, width), BF),
            jax.ShapeDtypeStruct((tile, 2 * head), F32),
        ),
        in_specs=[SMEM_SPEC] + [VMEM_SPEC] * 6,
        out_specs=(VMEM_SPEC,) * 2,
        scratch_shapes=[
            pltpu.VMEM((head, keys), BF),
            pltpu.VMEM((head, keys), BF),
            pltpu.VMEM((keys, head), BF),
            pltpu.VMEM((1, keys), F32),
        ],
        compiler_params=params(24),
        cost_estimate=cost(12 * tile * keys * width, 2 * (3 * tile * width + 4 * keys * head)),
        name="local_grads",
    )(info, q, g, att, log_total, kv_self, kv_anc)


def collect_kernel(table_ref, term_ref, keep_ref, came_ref, out_ref, sum_ref):
    nodes, depth = term_ref.shape[:2]
    width = term_ref.shape[3]
    owner = nodes * depth
    sum_ref[...] = jnp.zeros_like(sum_ref)

    def one_node(n, carry):
        slot = table_ref[owner + n]
        for k in range(depth):
            a = table_ref[n * depth + k]
            target = table_ref[owner + jnp.maximum(a, 0)]
            sum_ref[target] += jnp.where(a >= 0, term_ref[slot, k].astype(F32), 0.0)
        return carry

    lax.fori_loop(0, nodes, one_node, 0, unroll=16)
    out_ref[:, :, :width] = sum_ref[...].astype(BF)
    out_ref[:, :, width:] = (keep_ref[...].astype(F32) + came_ref[...].astype(F32)).astype(BF)


def collect(table, terms, keep, came):
    nodes, chunk, width = terms.shape[0], terms.shape[2], terms.shape[3]
    return pl.pallas_call(
        collect_kernel,
        out_shape=jax.ShapeDtypeStruct((nodes, chunk, width + keep.shape[2]), BF),
        in_specs=[SMEM_SPEC] + [VMEM_SPEC] * 3,
        out_specs=VMEM_SPEC,
        scratch_shapes=[pltpu.VMEM((nodes, chunk, width), F32)],
        compiler_params=params(),
        cost_estimate=cost(0, 4 * terms.size),
        name="collect",
    )(table, terms, keep, came)


def sum_parts_kernel(odd_ref, *refs):
    parts, (keep_ref, send_ref) = refs[:-2], refs[-2:]
    half = keep_ref.shape[2]
    for out_ref, first in ((keep_ref, odd_ref[0] * half), (send_ref, (1 - odd_ref[0]) * half)):
        at = pl.ds(pl.multiple_of(first, half), half)
        total = parts[0][at, :].astype(F32)
        for part in parts[1:]:
            total = total + part[at, :].astype(F32)
        out_ref[...] = total.astype(out_ref.dtype).T.reshape(out_ref.shape)


def sum_parts(odd, parts, nodes):
    width, rows = parts[0].shape
    shape = (nodes, rows // nodes, width // 2)
    return pl.pallas_call(
        sum_parts_kernel,
        out_shape=(jax.ShapeDtypeStruct(shape, BF), jax.ShapeDtypeStruct(shape, BF)),
        in_specs=[SMEM_SPEC] + [VMEM_SPEC] * len(parts),
        out_specs=(VMEM_SPEC, VMEM_SPEC),
        compiler_params=params(12),
        cost_estimate=cost(0, 10 * rows * width),
        name="sum_parts",
    )(odd, *parts)


def finish_kernel(weight_scale, got_ref, own_ref, gk_ref, gv_ref, gw_ref):
    tile, width = own_ref.shape
    head = width // 2
    total = got_ref[:, :, :width].reshape(tile, width).astype(F32) + own_ref[...]
    gk_ref[...] = total[:, :head].astype(BF)
    gv_ref[...] = total[:, head:].astype(BF)
    nodes, rows, half = got_ref.shape[0], got_ref.shape[1], got_ref.shape[2] - width
    sent = got_ref[:, :, width:].astype(F32).reshape(nodes // 2, 2, rows, half)
    sums = jnp.sum(sent, axis=0) * weight_scale
    gw_ref[:, :half] = sums[0]
    gw_ref[:, half:] = sums[1]


def finish(got, own, weight_scale):
    tile, width = own.shape
    return pl.pallas_call(
        lambda *refs: finish_kernel(weight_scale, *refs),
        out_shape=(
            jax.ShapeDtypeStruct((tile, width // 2), BF),
            jax.ShapeDtypeStruct((tile, width // 2), BF),
            jax.ShapeDtypeStruct((got.shape[1], 2 * (got.shape[2] - width)), F32),
        ),
        in_specs=[VMEM_SPEC] * 2,
        out_specs=(VMEM_SPEC,) * 3,
        compiler_params=params(),
        cost_estimate=cost(0, 4 * got.size),
        name="finish",
    )(got, own)


def ring(size, step):
    return [(i, (i + step) % size) for i in range(size)]


def per_device(queries, keys, values, grad_out, out_weight, ancestors, owner, lengths):
    q = queries[0, 0]
    tile, width = q.shape
    head = keys.shape[-1]
    seq = ("z", "y")
    nodes = lax.axis_size(seq)
    xs = lax.axis_size("x")
    core = lax.axis_index("core")
    x = lax.axis_index("x")
    me = lax.axis_index(seq).astype(jnp.int32).reshape(1)

    table = join_tables(ancestors[0], owner[0], lengths[0], me)
    kv_self = join(keys[0, 0], values[0, 0])
    kv_self, out_weight = lax.optimization_barrier((kv_self, out_weight))
    chunks = lax.all_to_all(kv_self, seq, 0, 0, tiled=True)
    def along(rows, step):
        return lax.ppermute(rows, "x", ring(xs, step))

    below, above = along(out_weight, 1), along(out_weight, xs - 1)
    mid = out_weight.shape[0] // 2
    below_low, above_high = below[:mid], above[mid:]
    grads = grad_out[0, 0]
    place = jnp.stack([x, core]).astype(jnp.int32)
    other = other_half(place, grads, xs)
    chunks, other, below, above, below_low, above_high = lax.optimization_barrier(
        (chunks, other, below, above, below_low, above_high)
    )
    weight = [[out_weight], [below], [along(below_low, 1), along(above_high, xs - 1)], [above]]
    sibling = lax.ppermute(other, "core", ring(2, 1))
    routed, info = route(table, chunks, ancestors.shape[2])
    kv_anc = lax.all_to_all(routed, seq, 0, 0, tiled=True)

    blocks = []
    for block in weight:
        blocks += [block, [lax.ppermute(rows, "core", ring(2, 1)) for rows in block]]
    grad_att = grad_attention(place, grads, blocks)

    att, att_low, log_total = forward(info, q, kv_self, kv_anc)
    att_sibling = lax.ppermute(att_low, "core", ring(2, 1))
    terms = ancestor_terms(info, q, grad_att, att, log_total, kv_anc)

    pieces = make_pieces(place, xs, grads, sibling, att_low, att_sibling)
    terms, pieces = lax.optimization_barrier((terms, pieces))
    own_piece, near, opposite_low, opposite_high = pieces
    from_below, from_above = along(opposite_low, 1), along(opposite_high, xs - 1)
    up, down = fold(near, from_below, from_above)
    parts = [own_piece, along(up, 1), along(down, xs - 1)]
    terms = lax.all_to_all(terms, seq, 0, 0, tiled=True)
    odd = lax.rem(lax.axis_index("y"), 2).astype(jnp.int32).reshape(1)
    grad_q, own = local_grads(info, q, grad_att, att, log_total, kv_self, kv_anc)
    keep, send = sum_parts(odd, parts, nodes)
    grad_q, own, send = lax.optimization_barrier((grad_q, own, send))
    came = lax.ppermute(send, "y", [(i, i ^ 1) for i in range(lax.axis_size("y"))])
    got = lax.all_to_all(collect(table, terms, keep, came), seq, 0, 0, tiled=True)
    token_count = 2 * xs * nodes * tile
    grad_k, grad_v, grad_w = finish(got, own, 1.0 / math.sqrt(token_count))
    return grad_q[None, None], grad_k[None, None], grad_v[None, None], grad_w


def solution(mesh):
    dp, seq = mesh.devices.shape
    fine = Mesh(mesh.devices.reshape(dp // 2, 2, seq // 4, 4), ("x", "core", "z", "y"))
    d, s = ("x", "core"), ("z", "y")
    placed = (
        P(d, s, None, None),
        P(d, s, None, None),
        P(d, s, None, None),
        P(d, s, None, None),
        P(d, None),
        P(d, None, None),
        P(d, None),
        P(d, None),
    )
    return jax.shard_map(
        per_device,
        mesh=fine,
        in_specs=placed,
        out_specs=(
            P(d, s, None, None),
            P(d, s, None, None),
            P(d, s, None, None),
            P(d + s, None),
        ),
        check_vma=False,
    )
```
